512 devices in a mesh: tm: 32 (over x_lo, z), space: 16 (over y, x_hi, core).
Axes of the slice: x: 4 (x_hi: 2, x_lo: 2; x = x_hi * 2 + x_lo), y: 4, z: 16, core: 2. Of those that a mesh axis runs over, the one named last changes fastest.
Arguments:
- latents: bfloat16 [64, 32, 160, 256], P('tm', 'space'), may hold values from -6 to 6
- grad_out: bfloat16 [64, 16, 80, 512], P('tm', 'space'), may hold values from -6 to 6
- w_spatial: bfloat16 [2304, 512], P('space'), may hold values from -0.125 to 0.125
- w_temporal: bfloat16 [1536, 512], P('space'), may hold values from -0.15625 to 0.15625
Outputs:
- grad_latents: bfloat16 [64, 32, 160, 256], P('tm', 'space')
- grad_temporal: float32 [1536, 512], P('space')
The draws below stay inside these ranges and needn't reach their ends.
All inputs are finite; a program needn't handle non-finite values.
Results may differ from the reference program's by a relative error of at most 0.0049.
Values may be sent and summed in bfloat16 or wider, within the bound.
A program may use at most 64 MiB of HBM per device.

```python
import jax
import jax.numpy as jnp
from jax import lax

IN_CH = 256
CH = 512
COLS = 80
FRAMES = 64
OUT_ROWS = 16


def block_levels(rng, extent, split, low, top_value):
    gain, own = 1.0, jax.random.fold_in(rng, 6)
    for position, parts in split:
        draws = jnp.exp(jax.random.uniform(jax.random.fold_in(own, position), (parts,), jnp.float32, low / len(split), top_value / len(split)))
        gain = gain * jnp.repeat(draws, extent[position] // parts).reshape([-1 if axis == position else 1 for axis in range(len(extent))])
    return gain


def centred(rng, dims, scale, limit, cuts=(), kind=jnp.bfloat16):
    entries = scale * jax.random.normal(rng, dims, jnp.float32)
    if cuts:
        entries = entries * block_levels(rng, dims, cuts, -0.22, 0.18)
    return jnp.clip(entries, -limit, limit).astype(kind)


def setup_inputs(seed: int = 0) -> dict:
    seeds = jax.random.split(jax.random.key(seed), 5)
    return {
        "latents": centred(seeds[0], (FRAMES, 2 * OUT_ROWS, 2 * COLS, IN_CH), 1.0, 6.0, ((0, 32), (1, 16))),
        "grad_out": centred(seeds[1], (FRAMES, OUT_ROWS, COLS, CH), 1.0, 6.0, ((0, 32), (1, 16))),
        "w_spatial": centred(seeds[2], (9 * IN_CH, CH), (9 * IN_CH) ** -0.5, 0.125, ((0, 16),)),
        "w_temporal": centred(seeds[3], (3 * CH, CH), (3 * CH) ** -0.5, 0.15625, ((0, 16),)),
    }


def window_taps(padded, rows_out, cols_out):
    pieces = []
    for row_tap in range(3):
        for col_tap in range(3):
            pieces.append(padded[..., row_tap:row_tap + 2 * rows_out:2, col_tap:col_tap + 2 * cols_out:2, :])
    return jnp.concatenate(pieces, axis=-1)


def column_fold(spread):
    shifted = jnp.concatenate([jnp.zeros_like(spread[..., :1, 2, :]), spread[..., :-1, 2, :]], axis=-2)
    even_cols = spread[..., 0, :] + shifted
    paired = jnp.stack([even_cols, spread[..., 1, :]], axis=-2)
    return paired.reshape(paired.shape[:-3] + (2 * paired.shape[-3], paired.shape[-1]))


def reference(latents, grad_out, w_spatial, w_temporal):
    padded = jnp.pad(latents, ((0, 0), (0, 1), (0, 1), (0, 0)))

    def forward_frame(one_frame):
        stacked = window_taps(one_frame, OUT_ROWS, COLS).reshape(-1, 9 * IN_CH)
        result = jnp.dot(stacked, w_spatial, preferred_element_type=jnp.float32)
        return result.astype(jnp.bfloat16).reshape(OUT_ROWS, COLS, CH)

    activations = lax.map(forward_frame, padded)
    acts_pad = jnp.concatenate([activations[:1], activations[:1], activations], axis=0)

    def add_frame(running, frame_at):
        stacked_acts = jnp.concatenate(
            [lax.dynamic_index_in_dim(acts_pad, frame_at + tap_index, 0, keepdims=False) for tap_index in range(3)],
            axis=-1).reshape(-1, 3 * CH)
        frame_grads = lax.dynamic_index_in_dim(grad_out, frame_at, 0, keepdims=False).reshape(-1, CH)
        return running + jnp.dot(stacked_acts.T, frame_grads, preferred_element_type=jnp.float32), None

    grad_temporal, unused = lax.scan(add_frame, jnp.zeros((3 * CH, CH), jnp.float32),
                                     jnp.arange(FRAMES, dtype=jnp.int32))

    flipped = w_temporal.reshape(3, CH, CH).transpose(0, 2, 1).reshape(3 * CH, CH)
    grad_pad = jnp.concatenate([grad_out, jnp.zeros((2, OUT_ROWS, COLS, CH), jnp.bfloat16)], axis=0)
    first_grads = grad_out[0].reshape(-1, CH)
    second_grads = grad_out[1].reshape(-1, CH)
    boundary = (jnp.dot(first_grads, flipped[:CH], preferred_element_type=jnp.float32)
                + jnp.dot(second_grads, flipped[:CH], preferred_element_type=jnp.float32)
                + jnp.dot(first_grads, flipped[CH:2 * CH], preferred_element_type=jnp.float32))

    def backward_frame(frame_at):
        stacked_grads = jnp.concatenate(
            [lax.dynamic_index_in_dim(grad_pad, frame_at + 2 - tap_index, 0, keepdims=False) for tap_index in range(3)],
            axis=-1).reshape(-1, 3 * CH)
        grad_acts = jnp.dot(stacked_grads, flipped, preferred_element_type=jnp.float32)
        grad_acts = grad_acts + jnp.where(frame_at == 0, boundary, jnp.zeros_like(boundary))
        grad_conv = grad_acts.astype(jnp.bfloat16)
        spread = lax.dot_general(grad_conv, w_spatial, (((1,), (1,)), ((), ())),
                                 preferred_element_type=jnp.float32).reshape(OUT_ROWS, COLS, 3, 3, IN_CH)
        folded = [column_fold(spread[:, :, tap_index]) for tap_index in range(3)]
        spilled = jnp.concatenate([jnp.zeros_like(folded[2][:1]), folded[2][:-1]], axis=0)
        paired = jnp.stack([folded[0] + spilled, folded[1]], axis=1)
        return paired.reshape(2 * OUT_ROWS, 2 * COLS, IN_CH).astype(jnp.bfloat16)

    grad_latents = lax.map(backward_frame, jnp.arange(FRAMES, dtype=jnp.int32))
    return grad_latents, grad_temporal
```

```python
import jax
import jax.numpy as jnp
from jax import lax
from jax.experimental import pallas as pl
from jax.experimental.pallas import tpu as pltpu
from jax.sharding import PartitionSpec as P

MESH = pl.DeviceIdType.MESH
F32 = jnp.float32
BF16 = jnp.bfloat16
SUBS = 2
ARRIVAL = (4, 1, 3, 5, 7, 2, 6)
RELAY = {4: 0, 1: 1, 3: 2, 5: 0, 7: 1, 2: 2, 6: 0}


def dot(a, b, ca, cb):
    return lax.dot_general(a, b, (((ca,), (cb,)), ((), ())), preferred_element_type=F32)


def place(x, y, z, c):
    return (lax.rem(x, 2) * 16 + z, y * 4 + (x // 2) * 2 + c)


def kernel(
    lat_hbm, gout_hbm, ws_hbm, wt_hbm, out_hbm, gt_hbm,
    lat, ws, wt, grads, eo, wide, patches, acts, tsum, tsend, trecv, zbuf,
    fin, fout, gap, gap_in, ga, shifted, po, po_in, outv,
    loc_sem, pair_s, pair_r, ext_s, ext_r, rel_s, rel_r, halo_s, halo_r,
    rs_s, rs_r, z_s, z_r, fin_s, fin_r,
):
    tm, sp = lax.axis_index("tm"), lax.axis_index("space")
    xl, z = tm // 16, lax.rem(tm, 16)
    c, chip = lax.rem(sp, 2), sp // 2
    y, xh = chip // 2, lax.rem(chip, 2)
    x = 2 * xh + xl
    par = lax.rem(xl + xh + z, 2)
    other = 1 - c
    z_up, z_down = lax.rem(z + 1, 16), lax.rem(z + 15, 16)

    partner = place(x, y, z, other)
    ups = [place(x, y, z_up, c), place(x, y, z_down, c), place(jnp.bitwise_xor(x, 1), y, z, c)]
    final_to = place(jnp.bitwise_xor(x, 1), y, z, xl)
    plane = []
    for dy in range(4):
        for dx in range(4):
            if dx or dy:
                plane.append((lax.rem(x + dx, 4), lax.rem(y + dy, 4)))
    tm_next, tm_prev = lax.rem(tm + 1, 32), lax.rem(tm + 31, 32)

    def half(index):
        return pl.ds(pl.multiple_of(index * 256, 256), 256)

    def rows(index, count):
        return pl.ds(pl.multiple_of(index * count, count), count)

    loads = [
        pltpu.make_async_copy(ws_hbm.at[:, half(c)], ws.at[rows(sp, 144)], loc_sem.at[0]),
        pltpu.make_async_copy(wt_hbm.at[:, half(c)], wt.at[rows(sp, 96)], loc_sem.at[1]),
        pltpu.make_async_copy(lat_hbm, lat, loc_sem.at[2]),
        pltpu.make_async_copy(gout_hbm.at[:, 0, :, half(c)], grads.at[pl.ds(0, 2), c], loc_sem.at[3]),
    ]
    for copy in loads:
        copy.start()

    barrier = pltpu.get_barrier_semaphore()
    greeted = [partner, ups[0], ups[1], place(jnp.bitwise_xor(x, 1), y, z, other), (tm_next, sp), (tm_next, chip * 2 + other)]
    greeted += [place(px, py, z, c) for px, py in plane]
    for device in greeted:
        pl.semaphore_signal(barrier, inc=1, device_id=device, device_id_type=MESH)
    pl.semaphore_wait(barrier, len(greeted))

    sent = []

    def send(src, dst, ssem, rsem, device):
        copy = pltpu.make_async_remote_copy(
            src_ref=src, dst_ref=dst, send_sem=ssem, recv_sem=rsem, device_id=device, device_id_type=MESH
        )
        copy.start()
        return copy

    pair_ws = send(ws_hbm.at[:, half(other)], ws.at[rows(sp, 144)], pair_s.at[0], pair_r.at[0], partner)
    pair_wt = send(wt_hbm.at[:, half(other)], wt.at[rows(sp, 96)], pair_s.at[1], pair_r.at[1], partner)
    pair_g = send(
        gout_hbm.at[:, 0, :, half(other)], grads.at[pl.ds(0, 2), c], pair_s.at[2], pair_r.at[2], partner
    )
    sent += [pair_ws, pair_wt, pair_g]

    def piece_chip(r):
        dxo, dy = r // 4, r % 4
        return lax.rem(y + 4 - dy, 4) * 2 + jnp.bitwise_xor(xh, dxo)

    def ext_device(r):
        dxo, dy = r // 4, r % 4
        tx = 3 - x if dxo else x
        return place(tx, lax.rem(y + dy, 4), z, c)

    mine = chip * 2 + par
    weights = ((ws, 144, 0), (wt, 96, 1))

    def ext_send(which):
        buf, count, lane = weights[which]
        return [
            send(buf.at[rows(mine, count)], buf.at[rows(mine, count)], ext_s.at[lane, r], ext_r.at[lane, r], ext_device(r))
            for r in ARRIVAL
        ]

    loads[0].wait()
    pair_ws.wait_recv()
    ext_ws = ext_send(0)
    loads[1].wait()
    pair_wt.wait_recv()
    ext_wt = ext_send(1)
    sent += ext_ws + ext_wt

    halo = []
    for h in range(2):
        halo.append(
            pltpu.make_async_remote_copy(
                src_ref=gout_hbm.at[:, 0, :, pl.ds(256 * h, 256)],
                dst_ref=grads.at[pl.ds(2, 2), c],
                send_sem=halo_s.at[h],
                recv_sem=halo_r.at[c],
                device_id=(tm_prev, chip * 2 + h),
                device_id_type=MESH,
            )
        )

    @pl.when(tm > 0)
    def _():
        for copy in halo:
            copy.start()

    loads[2].wait()
    for f in range(2):
        for r in range(2):
            for lane in range(2):
                across = pl.ds(128 * lane, 128)
                wide[lane] = lat[f, r, :, across].astype(F32)
                for odd in range(2):
                    eo[2 * c + r, f, odd, :, across] = wide[lane, pl.ds(odd, 80, 2), :].astype(BF16)
    pair_eo = send(eo.at[pl.ds(2 * c, 2)], eo.at[pl.ds(2 * c, 2)], pair_s.at[3], pair_r.at[3], partner)
    sent.append(pair_eo)
    pair_eo.wait_recv()

    prev_chip = lax.rem(chip + 7, 8)
    next_chip = lax.rem(chip + 1, 8)
    row_up = pltpu.make_async_remote_copy(
        src_ref=eo.at[0],
        dst_ref=eo.at[4],
        send_sem=halo_s.at[2],
        recv_sem=halo_r.at[2],
        device_id=(tm, prev_chip * 2 + c),
        device_id_type=MESH,
    )

    @pl.when(chip > 0)
    def _():
        row_up.start()

    @pl.when(chip == 7)
    def _():
        eo[4] = jnp.zeros_like(eo[4])

    @pl.when(tm == 31)
    def _():
        grads[2:4] = jnp.zeros_like(grads[2:4])

    last = lax.broadcasted_iota(jnp.int32, (80, 256), 0) == 79
    first = lax.broadcasted_iota(jnp.int32, (80, 256), 0) == 0

    def place_patch(f, i, r):
        row = 2 * i + r
        block = pl.ds((f * 2 + i) * 80, 80)
        even = eo[row, f, 0]
        moved = jnp.where(last, 0.0, pltpu.roll(even.astype(F32), 79, 0)).astype(BF16)
        patches[block, pl.ds(3 * r * 256, 256)] = even
        patches[block, pl.ds((3 * r + 1) * 256, 256)] = eo[row, f, 1]
        patches[block, pl.ds((3 * r + 2) * 256, 256)] = moved

    for f in range(2):
        for i in range(2):
            for r in range(3):
                if 2 * i + r < 4:
                    place_patch(f, i, r)

    def relay(which):
        buf, count, lane = weights[which]
        copies = []
        for at, r in enumerate(ARRIVAL):
            (ext_ws, ext_wt)[which][at].wait_recv()
            index = piece_chip(r) * 2 + par
            copies.append(
                send(buf.at[rows(index, count)], buf.at[rows(index, count)], rel_s.at[lane, r], rel_r.at[lane, r], ups[RELAY[r]])
            )
        return copies

    rel_ws = relay(0)

    @pl.when(chip < 7)
    def _():
        row_up.wait_recv()

    for f in range(2):
        place_patch(f, 1, 2)
    for copy in rel_ws:
        copy.wait_recv()

    acts[c] = jnp.dot(patches[...], ws[...], preferred_element_type=F32).astype(BF16)
    pair_a = send(acts.at[c], acts.at[c], pair_s.at[4], pair_r.at[4], partner)
    rel_wt = relay(1)
    sent += rel_ws + rel_wt + [pair_a]

    loads[3].wait()
    pair_g.wait_recv()

    @pl.when(tm < 31)
    def _():
        for core in range(2):
            pltpu.make_async_copy(grads.at[pl.ds(2, 2), core], grads.at[pl.ds(2, 2), core], halo_r.at[core]).wait()

    pair_a.wait_recv()

    def frames(start, count):
        return grads[start : start + count].reshape(count * 160, 256)

    for k in range(3):
        for h in range(2):
            tsum[pl.ds(k * 512 + h * 256, 256)] = dot(acts[h], frames(2 - k, 2), 0, 0)

    @pl.when(tm == 0)
    def _():
        for h in range(2):
            first_acts = acts[h, 0:160]
            zero = dot(first_acts, frames(0, 1), 0, 0)
            tsum[pl.ds(h * 256, 256)] += zero + dot(first_acts, frames(1, 1), 0, 0)
            tsum[pl.ds(512 + h * 256, 256)] += zero

    tsend[...] = tsum[...].astype(BF16)
    spread = []
    for at, (px, py) in enumerate(plane):
        block = 4 * py + px
        spread.append(
            send(tsend.at[rows(block, 96)], trecv.at[at], rs_s.at[at], rs_r.at[at], place(px, py, z, c))
        )
    sent += spread

    for copy in rel_wt:
        copy.wait_recv()
    for h in range(2):
        total = dot(frames(2, 2), wt[pl.ds(h * 256, 256)], 1, 1)
        total += dot(frames(1, 2), wt[pl.ds(512 + h * 256, 256)], 1, 1)
        total += dot(frames(0, 2), wt[pl.ds(1024 + h * 256, 256)], 1, 1)
        gap[h] = total

    @pl.when(tm == 0)
    def _():
        for h in range(2):
            more = dot(frames(0, 1), wt[pl.ds(h * 256, 256)], 1, 1)
            more += dot(frames(1, 1), wt[pl.ds(h * 256, 256)], 1, 1)
            more += dot(frames(0, 1), wt[pl.ds(512 + h * 256, 256)], 1, 1)
            gap[h, 0:160] += more

    pair_p = send(gap.at[other], gap_in, pair_s.at[5], pair_r.at[5], partner)
    sent.append(pair_p)
    pair_p.wait_recv()
    for f in range(2):
        for i in range(2):
            block = pl.ds((f * 2 + i) * 80, 80)
            ga[1 + i, f] = (gap[c, block] + gap_in[block]).astype(BF16)
    row_down = pltpu.make_async_remote_copy(
        src_ref=ga.at[2],
        dst_ref=ga.at[0],
        send_sem=halo_s.at[3],
        recv_sem=halo_r.at[3],
        device_id=(tm, next_chip * 2 + c),
        device_id_type=MESH,
    )

    @pl.when(chip < 7)
    def _():
        row_down.start()

    for copy in spread:
        copy.wait_recv()
    own_block = tsend[rows(4 * y + x, 96)].astype(F32)
    for at in range(15):
        own_block += trecv[at].astype(F32)
    zbuf[z] = own_block.astype(BF16)
    step_rows = 96 // SUBS
    ring = {}

    def ring_send(step, way, part):
        origin = lax.rem(z + 16 + (-(step - 1) if way == 0 else step - 1), 16)
        ref = zbuf.at[origin, pl.ds(part * step_rows, step_rows)]
        ring[step, way, part] = send(ref, ref, z_s.at[step, way, part], z_r.at[step, way, part], ups[way])

    def parts(step, way):
        if step < 8:
            return range(SUBS)
        return range(SUBS // 2) if way == 0 else range(SUBS // 2, SUBS)

    for part in range(SUBS):
        for way in range(2):
            ring_send(1, way, part)

    @pl.when(chip == 0)
    def _():
        ga[0] = jnp.zeros_like(ga[0])

    @pl.when(chip > 0)
    def _():
        row_down.wait_recv()

    def ring_step(step):
        for part in range(SUBS):
            for way in range(2):
                ring[step - 1, way, part].wait_recv()
                if part in parts(step, way):
                    ring_send(step, way, part)

    for row in range(3):
        for f in range(2):
            moved = jnp.where(first, 0.0, pltpu.roll(ga[row, f].astype(F32), 1, 0))
            shifted[row, f] = moved.astype(BF16)

    def tap(r, s):
        return ws[pl.ds((3 * r + s) * 256, 256)]

    cur, prev = ga[1:3].reshape(320, 256), ga[0:2].reshape(320, 256)
    cur_s, prev_s = shifted[1:3].reshape(320, 256), shifted[0:2].reshape(320, 256)

    def put(kind, value):
        po[0, kind] = value[:160]
        po[1, kind] = value[160:]

    ring_step(2)
    put(0, dot(cur, tap(0, 0), 1, 1) + dot(cur_s, tap(0, 2), 1, 1) + dot(prev, tap(2, 0), 1, 1) + dot(prev_s, tap(2, 2), 1, 1))
    ring_step(3)
    put(1, dot(cur, tap(0, 1), 1, 1) + dot(prev, tap(2, 1), 1, 1))
    ring_step(4)
    put(2, dot(cur, tap(1, 0), 1, 1) + dot(cur_s, tap(1, 2), 1, 1))
    put(3, dot(cur, tap(1, 1), 1, 1))
    pair_o = send(po.at[other], po_in, pair_s.at[6], pair_r.at[6], partner)
    sent.append(pair_o)
    ring_step(5)
    pair_o.wait_recv()

    def finish(f, r):
        block = pl.ds(f * 80, 80)
        for lane in range(2):
            across = pl.ds(128 * lane, 128)
            for odd in range(2):
                kind = 2 * r + odd
                wide[lane, pl.ds(odd, 80, 2), :] = po[c, kind, block, across] + po_in[kind, block, across]
            outv[f, r, :, across] = wide[lane].astype(BF16)

    finish(0, 0)
    finish(0, 1)
    ring_step(6)
    finish(1, 0)
    finish(1, 1)
    write_out = pltpu.make_async_copy(outv, out_hbm, loc_sem.at[4])
    write_out.start()
    ring_step(7)
    ring_step(8)
    for way in range(2):
        for part in parts(8, way):
            ring[8, way, part].wait_recv()
    sent += list(ring.values())
    total = zbuf[0].astype(F32)
    for at in range(1, 16):
        total += zbuf[at].astype(F32)
    fin[...] = total

    far = pltpu.make_async_remote_copy(
        src_ref=fin, dst_ref=fout.at[c], send_sem=fin_s.at[0], recv_sem=fin_r.at[c], device_id=final_to, device_id_type=MESH
    )
    near = pltpu.make_async_remote_copy(
        src_ref=fin, dst_ref=fout.at[c], send_sem=fin_s.at[1], recv_sem=fin_r.at[c], device_id=partner, device_id_type=MESH
    )
    far.start()

    def landed(h):
        pltpu.make_async_copy(fout.at[h], fout.at[h], fin_r.at[h]).wait()

    @pl.when(c == xl)
    def _():
        fout[c] = fin[...]
        landed(other)

    @pl.when(c != xl)
    def _():
        near.start()
        landed(0)
        landed(1)
        near.wait_send()

    writes = [
        pltpu.make_async_copy(fout.at[h], gt_hbm.at[:, pl.ds(256 * h, 256)], loc_sem.at[5 + h]) for h in range(2)
    ]
    for copy in writes:
        copy.start()
    far.wait_send()
    for copy in sent:
        copy.wait_send()

    @pl.when(tm > 0)
    def _():
        for copy in halo:
            copy.wait_send()

    @pl.when(chip > 0)
    def _():
        row_up.wait_send()

    @pl.when(chip < 7)
    def _():
        row_down.wait_send()

    write_out.wait()
    for copy in writes:
        copy.wait()


def local(latents, grad_out, w_spatial, w_temporal):
    dma = pltpu.SemaphoreType.DMA
    vmem = pltpu.VMEM
    return pl.pallas_call(
        kernel,
        out_shape=(
            jax.ShapeDtypeStruct(latents.shape, BF16),
            jax.ShapeDtypeStruct((96, 512), F32),
        ),
        in_specs=[pl.BlockSpec(memory_space=pl.ANY)] * 4,
        out_specs=[pl.BlockSpec(memory_space=pl.ANY)] * 2,
        scratch_shapes=[
            vmem((2, 2, 160, 256), BF16),
            vmem((2304, 256), BF16),
            vmem((1536, 256), BF16),
            vmem((4, 2, 80, 256), BF16),
            vmem((5, 2, 2, 80, 256), BF16),
            vmem((2, 160, 128), F32),
            vmem((320, 2304), BF16),
            vmem((2, 320, 256), BF16),
            vmem((1536, 256), F32),
            vmem((1536, 256), BF16),
            vmem((15, 96, 256), BF16),
            vmem((16, 96, 256), BF16),
            vmem((96, 256), F32),
            vmem((2, 96, 256), F32),
            vmem((2, 320, 256), F32),
            vmem((320, 256), F32),
            vmem((3, 2, 80, 256), BF16),
            vmem((3, 2, 80, 256), BF16),
            vmem((2, 4, 160, 256), F32),
            vmem((4, 160, 256), F32),
            vmem((2, 2, 160, 256), BF16),
            dma((7,)),
            dma((7,)),
            dma((7,)),
            dma((2, 8)),
            dma((2, 8)),
            dma((2, 8)),
            dma((2, 8)),
            dma((4,)),
            dma((4,)),
            dma((15,)),
            dma((15,)),
            dma((9, 2, SUBS)),
            dma((9, 2, SUBS)),
            dma((2,)),
            dma((2,)),
        ],
        compiler_params=pltpu.CompilerParams(
            collective_id=0, has_side_effects=True, vmem_limit_bytes=48 * 2**20
        ),
    )(latents, grad_out, w_spatial, w_temporal)


def solution(mesh):
    return jax.shard_map(
        local,
        mesh=mesh,
        in_specs=(
            P("tm", "space", None, None),
            P("tm", "space", None, None),
            P("space", None),
            P("space", None),
        ),
        out_specs=(P("tm", "space", None, None), P("space", None)),
        check_vma=False,
    )
```

```python
import jax
import jax.numpy as jnp
from jax import lax
from jax.experimental import pallas as pl
from jax.experimental.pallas import tpu as pltpu
from jax.sharding import PartitionSpec as P

MESH = pl.DeviceIdType.MESH
F32 = jnp.float32
BF16 = jnp.bfloat16
ARRIVAL = (4, 1, 3, 5, 7, 2, 6)
RELAY = {4: 0, 1: 1, 3: 2, 5: 0, 7: 1, 2: 2, 6: 0}


def dot(a, b, ca, cb):
    return lax.dot_general(a, b, (((ca,), (cb,)), ((), ())), preferred_element_type=F32)


def place(x, y, z, c):
    return (lax.rem(x, 2) * 16 + z, y * 4 + (x // 2) * 2 + c)


def kernel(
    lat_hbm, gout_hbm, ws_hbm, wt_hbm, outv, gt,
    lat, ws, wt, grads, eo, wide, patches, acts, tsum, tsend, trecv,
    near, near_in, far, quad, fout, gap, gap_in, ga, shifted, po, po_in,
    loc_sem, pair_s, pair_r, ext_s, ext_r, rel_s, rel_r, halo_s, halo_r,
    rs_s, rs_r, near_s, near_r, far_s, far_r, fin_s, fin_r, known,
):
    tm, sp = lax.axis_index("tm"), lax.axis_index("space")
    xl, z = tm // 16, lax.rem(tm, 16)
    c, chip = lax.rem(sp, 2), sp // 2
    y, xh = chip // 2, lax.rem(chip, 2)
    x = 2 * xh + xl
    par = lax.rem(xl + xh + z, 2)
    other = 1 - c
    z_up, z_down = lax.rem(z + 1, 16), lax.rem(z + 15, 16)

    partner = place(x, y, z, other)
    ups = [place(x, y, z_up, c), place(x, y, z_down, c), place(jnp.bitwise_xor(x, 1), y, z, c)]
    zq, zr = z // 4, lax.rem(z, 4)
    plane = []
    for dy in range(4):
        for dx in range(4):
            if dx or dy:
                plane.append((lax.rem(x + dx, 4), lax.rem(y + dy, 4)))
    tm_next, tm_prev = lax.rem(tm + 1, 32), lax.rem(tm + 31, 32)

    def half(index):
        return pl.ds(pl.multiple_of(index * 256, 256), 256)

    def rows(index, count):
        return pl.ds(pl.multiple_of(index * count, count), count)

    loads = [
        pltpu.make_async_copy(ws_hbm.at[:, half(c)], ws.at[rows(sp, 144)], loc_sem.at[0]),
        pltpu.make_async_copy(wt_hbm.at[:, half(c)], wt.at[rows(sp, 96)], loc_sem.at[1]),
        pltpu.make_async_copy(lat_hbm, lat, loc_sem.at[2]),
        pltpu.make_async_copy(gout_hbm.at[:, 0, :, half(c)], grads.at[pl.ds(0, 2), c], loc_sem.at[3]),
    ]
    for copy in loads:
        copy.start()

    barrier = pltpu.get_barrier_semaphore()
    greeted = [partner, ups[0], ups[1], place(jnp.bitwise_xor(x, 1), y, z, other), (tm_next, sp), (tm_next, chip * 2 + other)]
    greeted += [place(px, py, z, c) for px, py in plane]
    for device in greeted:
        pl.semaphore_signal(barrier, inc=1, device_id=device, device_id_type=MESH)
    pl.semaphore_wait(barrier, len(greeted))

    def meet(stage):
        for way in (1, -1):
            there = place(x, y, lax.rem(z + 16 + way * 2**stage, 16), c)
            pl.semaphore_signal(known.at[stage], inc=1, device_id=there, device_id_type=MESH)

    def met(stage):
        pl.semaphore_wait(known.at[stage], 2)

    meet(0)
    sent = []

    def send(src, dst, ssem, rsem, device):
        copy = pltpu.make_async_remote_copy(
            src_ref=src, dst_ref=dst, send_sem=ssem, recv_sem=rsem, device_id=device, device_id_type=MESH
        )
        copy.start()
        return copy

    pair_ws = send(ws_hbm.at[:, half(other)], ws.at[rows(sp, 144)], pair_s.at[0], pair_r.at[0], partner)
    pair_wt = send(wt_hbm.at[:, half(other)], wt.at[rows(sp, 96)], pair_s.at[1], pair_r.at[1], partner)
    pair_g = send(
        gout_hbm.at[:, 0, :, half(other)], grads.at[pl.ds(0, 2), c], pair_s.at[2], pair_r.at[2], partner
    )
    sent += [pair_ws, pair_wt, pair_g]

    def piece_chip(r):
        dxo, dy = r // 4, r % 4
        return lax.rem(y + 4 - dy, 4) * 2 + jnp.bitwise_xor(xh, dxo)

    def ext_device(r):
        dxo, dy = r // 4, r % 4
        tx = 3 - x if dxo else x
        return place(tx, lax.rem(y + dy, 4), z, c)

    mine = chip * 2 + par
    weights = ((ws, 144, 0), (wt, 96, 1))

    def ext_send(which):
        buf, count, lane = weights[which]
        return [
            send(buf.at[rows(mine, count)], buf.at[rows(mine, count)], ext_s.at[lane, r], ext_r.at[lane, r], ext_device(r))
            for r in ARRIVAL
        ]

    loads[0].wait()
    pair_ws.wait_recv()
    ext_ws = ext_send(0)
    sent += ext_ws

    halo = []
    for h in range(2):
        halo.append(
            pltpu.make_async_remote_copy(
                src_ref=gout_hbm.at[:, 0, :, pl.ds(256 * h, 256)],
                dst_ref=grads.at[pl.ds(2, 2), c],
                send_sem=halo_s.at[h],
                recv_sem=halo_r.at[c],
                device_id=(tm_prev, chip * 2 + h),
                device_id_type=MESH,
            )
        )

    @pl.when(tm > 0)
    def _():
        for copy in halo:
            copy.start()

    met(0)
    meet(1)

    loads[2].wait()
    for f in range(2):
        for r in range(2):
            for lane in range(2):
                across = pl.ds(128 * lane, 128)
                wide[lane] = lat[f, r, :, across].astype(F32)
                for odd in range(2):
                    eo[2 * c + r, f, odd, :, across] = wide[lane, pl.ds(odd, 80, 2), :].astype(BF16)
    pair_eo = send(eo.at[pl.ds(2 * c, 2)], eo.at[pl.ds(2 * c, 2)], pair_s.at[3], pair_r.at[3], partner)
    sent.append(pair_eo)
    pair_eo.wait_recv()

    prev_chip = lax.rem(chip + 7, 8)
    next_chip = lax.rem(chip + 1, 8)
    row_up = pltpu.make_async_remote_copy(
        src_ref=eo.at[0],
        dst_ref=eo.at[4],
        send_sem=halo_s.at[2],
        recv_sem=halo_r.at[2],
        device_id=(tm, prev_chip * 2 + c),
        device_id_type=MESH,
    )

    @pl.when(chip > 0)
    def _():
        row_up.start()

    @pl.when(chip == 7)
    def _():
        eo[4] = jnp.zeros_like(eo[4])

    @pl.when(tm == 31)
    def _():
        grads[2:4] = jnp.zeros_like(grads[2:4])

    last = lax.broadcasted_iota(jnp.int32, (80, 256), 0) == 79
    first = lax.broadcasted_iota(jnp.int32, (80, 256), 0) == 0

    def place_patch(f, i, r):
        row = 2 * i + r
        block = pl.ds((f * 2 + i) * 80, 80)
        even = eo[row, f, 0]
        moved = jnp.where(last, 0.0, pltpu.roll(even.astype(F32), 79, 0)).astype(BF16)
        patches[block, pl.ds(3 * r * 256, 256)] = even
        patches[block, pl.ds((3 * r + 1) * 256, 256)] = eo[row, f, 1]
        patches[block, pl.ds((3 * r + 2) * 256, 256)] = moved

    for f in range(2):
        for i in range(2):
            for r in range(3):
                if 2 * i + r < 4:
                    place_patch(f, i, r)

    met(1)
    meet(2)

    def relay(which, arriving):
        buf, count, lane = weights[which]
        copies = []
        for at, r in enumerate(ARRIVAL):
            arriving[at].wait_recv()
            index = piece_chip(r) * 2 + par
            copies.append(
                send(buf.at[rows(index, count)], buf.at[rows(index, count)], rel_s.at[lane, r], rel_r.at[lane, r], ups[RELAY[r]])
            )
        return copies

    rel_ws = relay(0, ext_ws)
    loads[1].wait()
    pair_wt.wait_recv()
    ext_wt = ext_send(1)
    sent += rel_ws + ext_wt

    @pl.when(chip < 7)
    def _():
        row_up.wait_recv()

    for f in range(2):
        place_patch(f, 1, 2)
    for copy in rel_ws:
        copy.wait_recv()

    acts[c] = jnp.dot(patches[...], ws[...], preferred_element_type=F32).astype(BF16)
    pair_a = send(acts.at[c], acts.at[c], pair_s.at[4], pair_r.at[4], partner)
    sent.append(pair_a)

    loads[3].wait()
    pair_g.wait_recv()

    @pl.when(tm < 31)
    def _():
        for core in range(2):
            pltpu.make_async_copy(grads.at[pl.ds(2, 2), core], grads.at[pl.ds(2, 2), core], halo_r.at[core]).wait()

    pair_a.wait_recv()

    def frames(start, count):
        return grads[start : start + count].reshape(count * 160, 256)

    for k in range(3):
        for h in range(2):
            tsum[pl.ds(k * 512 + h * 256, 256)] = dot(acts[h], frames(2 - k, 2), 0, 0)

    @pl.when(tm == 0)
    def _():
        for h in range(2):
            first_acts = acts[h, 0:160]
            zero = dot(first_acts, frames(0, 1), 0, 0)
            tsum[pl.ds(h * 256, 256)] += zero + dot(first_acts, frames(1, 1), 0, 0)
            tsum[pl.ds(512 + h * 256, 256)] += zero

    tsend[...] = tsum[...].astype(BF16)
    spread = []
    for at, (px, py) in enumerate(plane):
        block = 4 * py + px
        spread.append(
            send(tsend.at[rows(block, 96)], trecv.at[at], rs_s.at[at], rs_r.at[at], place(px, py, z, c))
        )
    sent += spread

    rel_wt = relay(1, ext_wt)
    sent += rel_wt
    for copy in rel_wt:
        copy.wait_recv()
    for h in range(2):
        total = dot(frames(2, 2), wt[pl.ds(h * 256, 256)], 1, 1)
        total += dot(frames(1, 2), wt[pl.ds(512 + h * 256, 256)], 1, 1)
        total += dot(frames(0, 2), wt[pl.ds(1024 + h * 256, 256)], 1, 1)
        gap[h] = total

    @pl.when(tm == 0)
    def _():
        for h in range(2):
            more = dot(frames(0, 1), wt[pl.ds(h * 256, 256)], 1, 1)
            more += dot(frames(1, 1), wt[pl.ds(h * 256, 256)], 1, 1)
            more += dot(frames(0, 1), wt[pl.ds(512 + h * 256, 256)], 1, 1)
            gap[h, 0:160] += more

    pair_p = send(gap.at[other], gap_in, pair_s.at[5], pair_r.at[5], partner)
    sent.append(pair_p)

    for copy in spread:
        copy.wait_recv()
    block_sum = tsend[rows(4 * y + x, 96)].astype(F32)
    for at in range(15):
        block_sum += trecv[at].astype(F32)
    for q in range(4):
        near[q] = block_sum[48 * (q // 2) : 48 * (q // 2) + 48, 128 * (q % 2) : 128 * (q % 2) + 128].astype(BF16)
    near_copies = []
    for j in range(1, 4):
        to = lax.rem(zr + j, 4)
        near_copies.append(
            send(near.at[to], near_in.at[zr], near_s.at[j], near_r.at[j], place(x, y, 4 * zq + to, c))
        )
    sent += near_copies
    near_in[zr] = near[zr]

    pair_p.wait_recv()
    for f in range(2):
        for i in range(2):
            block = pl.ds((f * 2 + i) * 80, 80)
            ga[1 + i, f] = (gap[c, block] + gap_in[block]).astype(BF16)
    row_down = pltpu.make_async_remote_copy(
        src_ref=ga.at[2],
        dst_ref=ga.at[0],
        send_sem=halo_s.at[3],
        recv_sem=halo_r.at[3],
        device_id=(tm, next_chip * 2 + c),
        device_id_type=MESH,
    )

    @pl.when(chip < 7)
    def _():
        row_down.start()

    for copy in near_copies:
        copy.wait_recv()
    group_sum = near_in[0].astype(F32)
    for at in range(1, 4):
        group_sum += near_in[at].astype(F32)
    far[zq] = group_sum.astype(BF16)
    met(2)
    far_copies = []
    for j in range(1, 4):
        to = lax.rem(zq + j, 4)
        far_copies.append(
            send(far.at[zq], far.at[zq], far_s.at[j], far_r.at[j], place(x, y, 4 * to + zr, c))
        )
    sent += far_copies

    @pl.when(chip == 0)
    def _():
        ga[0] = jnp.zeros_like(ga[0])

    @pl.when(chip > 0)
    def _():
        row_down.wait_recv()

    for row in range(3):
        for f in range(2):
            moved = jnp.where(first, 0.0, pltpu.roll(ga[row, f].astype(F32), 1, 0))
            shifted[row, f] = moved.astype(BF16)

    def tap(r, s):
        return ws[pl.ds((3 * r + s) * 256, 256)]

    cur, prev = ga[1:3].reshape(320, 256), ga[0:2].reshape(320, 256)
    cur_s, prev_s = shifted[1:3].reshape(320, 256), shifted[0:2].reshape(320, 256)

    def put(kind, value):
        po[0, kind] = value[:160]
        po[1, kind] = value[160:]

    put(0, dot(cur, tap(0, 0), 1, 1) + dot(cur_s, tap(0, 2), 1, 1) + dot(prev, tap(2, 0), 1, 1) + dot(prev_s, tap(2, 2), 1, 1))
    put(1, dot(cur, tap(0, 1), 1, 1) + dot(prev, tap(2, 1), 1, 1))
    put(2, dot(cur, tap(1, 0), 1, 1) + dot(cur_s, tap(1, 2), 1, 1))
    put(3, dot(cur, tap(1, 1), 1, 1))
    pair_o = send(po.at[other], po_in, pair_s.at[6], pair_r.at[6], partner)
    sent.append(pair_o)

    def finish(f, r):
        block = pl.ds(f * 80, 80)
        for lane in range(2):
            across = pl.ds(128 * lane, 128)
            for odd in range(2):
                kind = 2 * r + odd
                wide[lane, pl.ds(odd, 80, 2), :] = po[c, kind, block, across] + po_in[kind, block, across]
            outv[f, r, :, across] = wide[lane].astype(BF16)

    for copy in far_copies:
        copy.wait_recv()
    quarter = far[0].astype(F32)
    for at in range(1, 4):
        quarter += far[at].astype(F32)
    quad[...] = quarter
    fin_copies = []
    for flip in range(2):
        for j in range(4):
            if flip or j:
                to = place(jnp.bitwise_xor(x, flip), y, 4 * zq + lax.rem(zr + j, 4), xl)
                fin_copies.append(send(quad, fout.at[c, zr], fin_s.at[flip, j], fin_r.at[c, zr], to))
    here = pltpu.make_async_copy(quad, fout.at[c, zr], fin_r.at[c, zr])
    beside = pltpu.make_async_remote_copy(
        src_ref=quad, dst_ref=fout.at[c, zr], send_sem=fin_s.at[0, 0], recv_sem=fin_r.at[c, zr], device_id=partner, device_id_type=MESH
    )

    @pl.when(c == xl)
    def _():
        here.start()

    @pl.when(c != xl)
    def _():
        beside.start()

    pair_o.wait_recv()
    for f in range(2):
        for r in range(2):
            finish(f, r)

    for h in range(2):
        for q in range(4):
            pltpu.make_async_copy(fout.at[h, q], fout.at[h, q], fin_r.at[h, q]).wait()
            gt[pl.ds(48 * (q // 2), 48), pl.ds(256 * h + 128 * (q % 2), 128)] = fout[h, q]

    for copy in sent + fin_copies:
        copy.wait_send()

    @pl.when(c != xl)
    def _():
        beside.wait_send()

    @pl.when(tm > 0)
    def _():
        for copy in halo:
            copy.wait_send()

    @pl.when(chip > 0)
    def _():
        row_up.wait_send()

    @pl.when(chip < 7)
    def _():
        row_down.wait_send()


def local(latents, grad_out, w_spatial, w_temporal):
    dma = pltpu.SemaphoreType.DMA
    vmem = pltpu.VMEM
    return pl.pallas_call(
        kernel,
        out_shape=(
            jax.ShapeDtypeStruct(latents.shape, BF16),
            jax.ShapeDtypeStruct((96, 512), F32),
        ),
        in_specs=[pl.BlockSpec(memory_space=pl.ANY)] * 4,
        out_specs=[pl.BlockSpec(memory_space=pltpu.VMEM)] * 2,
        scratch_shapes=[
            vmem((2, 2, 160, 256), BF16),
            vmem((2304, 256), BF16),
            vmem((1536, 256), BF16),
            vmem((4, 2, 80, 256), BF16),
            vmem((5, 2, 2, 80, 256), BF16),
            vmem((2, 160, 128), F32),
            vmem((320, 2304), BF16),
            vmem((2, 320, 256), BF16),
            vmem((1536, 256), F32),
            vmem((1536, 256), BF16),
            vmem((15, 96, 256), BF16),
            vmem((4, 48, 128), BF16),
            vmem((4, 48, 128), BF16),
            vmem((4, 48, 128), BF16),
            vmem((48, 128), F32),
            vmem((2, 4, 48, 128), F32),
            vmem((2, 320, 256), F32),
            vmem((320, 256), F32),
            vmem((3, 2, 80, 256), BF16),
            vmem((3, 2, 80, 256), BF16),
            vmem((2, 4, 160, 256), F32),
            vmem((4, 160, 256), F32),
            dma((4,)),
            dma((7,)),
            dma((7,)),
            dma((2, 8)),
            dma((2, 8)),
            dma((2, 8)),
            dma((2, 8)),
            dma((4,)),
            dma((4,)),
            dma((15,)),
            dma((15,)),
            dma((4,)),
            dma((4,)),
            dma((4,)),
            dma((4,)),
            dma((2, 4)),
            dma((2, 4)),
            pltpu.SemaphoreType.REGULAR((3,)),
        ],
        compiler_params=pltpu.CompilerParams(
            collective_id=0, has_side_effects=True, vmem_limit_bytes=60 * 2**20
        ),
    )(latents, grad_out, w_spatial, w_temporal)


def solution(mesh):
    return jax.shard_map(
        local,
        mesh=mesh,
        in_specs=(
            P("tm", "space", None, None),
            P("tm", "space", None, None),
            P("space", None),
            P("space", None),
        ),
        out_specs=(P("tm", "space", None, None), P("space", None)),
        check_vma=False,
    )
```

```python
import jax
import jax.numpy as jnp
from jax import lax
from jax.experimental import pallas as pl
from jax.experimental.pallas import tpu as pltpu
from jax.sharding import PartitionSpec as P

MESH = pl.DeviceIdType.MESH
F32 = jnp.float32
BF16 = jnp.bfloat16
FAR = (2, 5, 7, 6)
NEAR = (4, 1, 3)


def dot(a, b, ca, cb):
    return lax.dot_general(a, b, (((ca,), (cb,)), ((), ())), preferred_element_type=F32)


def place(x, y, z, c):
    return (lax.rem(x, 2) * 16 + z, y * 4 + (x // 2) * 2 + c)


def kernel(
    lat_hbm, gout_hbm, ws_hbm, wt_hbm, outv, gt,
    lat, ws, wt, grads, eo, wide, patches, acts, tsum, tsend, trecv,
    ws_other, wt_other, g_other, near, near_in, far, quad, fout, gap, gap_in, ga, shifted, po, po_in,
    loc_sem, pair_s, pair_r, ext_s, ext_r, rel_s, rel_r, halo_s, halo_r,
    rs_s, rs_r, near_s, near_r, far_s, far_r, fin_s, fin_r, known,
):
    tm, sp = lax.axis_index("tm"), lax.axis_index("space")
    xl, z = tm // 16, lax.rem(tm, 16)
    c, chip = lax.rem(sp, 2), sp // 2
    y, xh = chip // 2, lax.rem(chip, 2)
    x = 2 * xh + xl
    par = lax.rem(xl + xh + z, 2)
    other = 1 - c
    z_up, z_down = lax.rem(z + 1, 16), lax.rem(z + 15, 16)

    partner = place(x, y, z, other)
    ups = [place(x, y, z_up, c), place(x, y, z_down, c), place(jnp.bitwise_xor(x, 1), y, z, c)]
    zq, zr = z // 4, lax.rem(z, 4)
    plane = []
    for dy in range(4):
        for dx in range(4):
            if dx or dy:
                plane.append((lax.rem(x + dx, 4), lax.rem(y + dy, 4)))
    tm_next, tm_prev = lax.rem(tm + 1, 32), lax.rem(tm + 31, 32)

    def half(index):
        return pl.ds(pl.multiple_of(index * 256, 256), 256)

    def rows(index, count):
        return pl.ds(pl.multiple_of(index * count, count), count)

    loads = [
        pltpu.make_async_copy(ws_hbm.at[:, half(c)], ws.at[rows(sp, 144)], loc_sem.at[0]),
        pltpu.make_async_copy(wt_hbm.at[:, half(c)], wt.at[rows(sp, 96)], loc_sem.at[1]),
        pltpu.make_async_copy(lat_hbm, lat, loc_sem.at[2]),
        pltpu.make_async_copy(gout_hbm.at[:, 0, :, half(c)], grads.at[pl.ds(0, 2), c], loc_sem.at[3]),
        pltpu.make_async_copy(ws_hbm.at[:, half(other)], ws_other, loc_sem.at[4]),
        pltpu.make_async_copy(wt_hbm.at[:, half(other)], wt_other, loc_sem.at[5]),
        pltpu.make_async_copy(gout_hbm.at[:, 0, :, half(other)], g_other, loc_sem.at[6]),
    ]
    for at in (4, 0, 2, 5, 1, 6, 3):
        loads[at].start()

    barrier = pltpu.get_barrier_semaphore()
    greeted = [partner, ups[0], ups[1], place(jnp.bitwise_xor(x, 1), y, z, other), (tm_next, sp), (tm_next, chip * 2 + other)]
    greeted += [place(px, py, z, c) for px, py in plane]
    for device in greeted:
        pl.semaphore_signal(barrier, inc=1, device_id=device, device_id_type=MESH)
    pl.semaphore_wait(barrier, len(greeted))

    def meet(stage):
        for way in (1, -1):
            there = place(x, y, lax.rem(z + 16 + way * 2**stage, 16), c)
            pl.semaphore_signal(known.at[stage], inc=1, device_id=there, device_id_type=MESH)

    def met(stage):
        pl.semaphore_wait(known.at[stage], 2)

    meet(0)
    sent = []

    def send(src, dst, ssem, rsem, device):
        copy = pltpu.make_async_remote_copy(
            src_ref=src, dst_ref=dst, send_sem=ssem, recv_sem=rsem, device_id=device, device_id_type=MESH
        )
        copy.start()
        return copy

    loads[4].wait()
    pair_ws = send(ws_other, ws.at[rows(sp, 144)], pair_s.at[0], pair_r.at[0], partner)
    loads[5].wait()
    pair_wt = send(wt_other, wt.at[rows(sp, 96)], pair_s.at[1], pair_r.at[1], partner)

    def piece_chip(r):
        dxo, dy = r // 4, r % 4
        return lax.rem(y + 4 - dy, 4) * 2 + jnp.bitwise_xor(xh, dxo)

    def ext_device(r):
        dxo, dy = r // 4, r % 4
        tx = 3 - x if dxo else x
        return place(tx, lax.rem(y + dy, 4), z, c)

    weights = ((ws, 144), (wt, 96))

    def piece(which, index, part=None):
        buf, count = weights[which]
        if part is None:
            return buf.at[rows(index, count)]
        third = count // 3
        return buf.at[pl.ds(pl.multiple_of(index * count + part * third, third), third)]

    def ext_copies(which, group):
        jobs = [(r, r) for r in FAR + NEAR] if group == 0 else [(r, 8 + at) for at, r in enumerate(NEAR)]
        ref = piece(which, chip * 2 + (par if group == 0 else 1 - par))
        return [
            pltpu.make_async_remote_copy(
                src_ref=ref,
                dst_ref=ref,
                send_sem=ext_s.at[which, slot],
                recv_sem=ext_r.at[which, slot],
                device_id=ext_device(r),
                device_id_type=MESH,
            )
            for r, slot in jobs
        ]

    ext = [[ext_copies(which, group) for group in range(2)] for which in range(2)]
    for which in range(2):
        for group in range(2):
            sent += ext[which][group]
    loads[0].wait()

    @pl.when(c == par)
    def _():
        for copy in ext[0][0]:
            copy.start()

    pair_ws.wait_recv()

    @pl.when(c != par)
    def _():
        for copy in ext[0][0]:
            copy.start()

    for copy in ext[0][1]:
        copy.start()

    loads[6].wait()
    pair_g = send(g_other, grads.at[pl.ds(0, 2), c], pair_s.at[2], pair_r.at[2], partner)
    sent += [pair_ws, pair_wt, pair_g]

    halo = []
    for h in range(2):
        halo.append(
            pltpu.make_async_remote_copy(
                src_ref=gout_hbm.at[:, 0, :, pl.ds(256 * h, 256)],
                dst_ref=grads.at[pl.ds(2, 2), c],
                send_sem=halo_s.at[h],
                recv_sem=halo_r.at[c],
                device_id=(tm_prev, chip * 2 + h),
                device_id_type=MESH,
            )
        )

    @pl.when(tm > 0)
    def _():
        for copy in halo:
            copy.start()

    met(0)
    meet(1)

    loads[2].wait()
    for f in range(2):
        for r in range(2):
            for lane in range(2):
                across = pl.ds(128 * lane, 128)
                wide[lane] = lat[f, r, :, across].astype(F32)
                for odd in range(2):
                    eo[2 * c + r, f, odd, :, across] = wide[lane, pl.ds(odd, 80, 2), :].astype(BF16)
    pair_eo = send(eo.at[pl.ds(2 * c, 2)], eo.at[pl.ds(2 * c, 2)], pair_s.at[3], pair_r.at[3], partner)
    sent.append(pair_eo)
    pair_eo.wait_recv()

    prev_chip = lax.rem(chip + 7, 8)
    next_chip = lax.rem(chip + 1, 8)
    row_up = pltpu.make_async_remote_copy(
        src_ref=eo.at[0],
        dst_ref=eo.at[4],
        send_sem=halo_s.at[2],
        recv_sem=halo_r.at[2],
        device_id=(tm, prev_chip * 2 + c),
        device_id_type=MESH,
    )

    @pl.when(chip > 0)
    def _():
        row_up.start()

    @pl.when(chip == 7)
    def _():
        eo[4] = jnp.zeros_like(eo[4])

    @pl.when(tm == 31)
    def _():
        grads[2:4] = jnp.zeros_like(grads[2:4])

    last = lax.broadcasted_iota(jnp.int32, (80, 256), 0) == 79
    first = lax.broadcasted_iota(jnp.int32, (80, 256), 0) == 0

    def place_patch(f, i, r):
        row = 2 * i + r
        block = pl.ds((f * 2 + i) * 80, 80)
        even = eo[row, f, 0]
        moved = jnp.where(last, 0.0, pltpu.roll(even.astype(F32), 79, 0)).astype(BF16)
        patches[block, pl.ds(3 * r * 256, 256)] = even
        patches[block, pl.ds((3 * r + 1) * 256, 256)] = eo[row, f, 1]
        patches[block, pl.ds((3 * r + 2) * 256, 256)] = moved

    for f in range(2):
        for i in range(2):
            for r in range(3):
                if 2 * i + r < 4:
                    place_patch(f, i, r)

    met(1)
    meet(2)

    def relay(which):
        for at, r in enumerate(FAR):
            ext[which][0][at].wait_recv()
            index = piece_chip(r) * 2 + par
            for part in range(3):
                ref = piece(which, index, part) if at == 3 else piece(which, index)
                if at == 3 or part == at:
                    slot = 3 + part if at == 3 else at
                    sent.append(send(ref, ref, rel_s.at[which, slot], rel_r.at[which, slot], ups[part]))

    def all_here(which):
        for copy in ext[which][0][4:] + ext[which][1]:
            copy.wait_recv()
        for at, r in enumerate(FAR):
            index = piece_chip(r) * 2 + 1 - par
            if at < 3:
                ref = piece(which, index)
                pltpu.make_async_copy(ref, ref, rel_r.at[which, at]).wait()
            else:
                for part in range(3):
                    ref = piece(which, index, part)
                    pltpu.make_async_copy(ref, ref, rel_r.at[which, 3 + part]).wait()

    relay(0)
    loads[1].wait()
    pair_wt.wait_recv()
    for copy in ext[1][0] + ext[1][1]:
        copy.start()

    @pl.when(chip < 7)
    def _():
        row_up.wait_recv()

    for f in range(2):
        place_patch(f, 1, 2)
    all_here(0)

    acts[c] = jnp.dot(patches[...], ws[...], preferred_element_type=F32).astype(BF16)
    pair_a = send(acts.at[c], acts.at[c], pair_s.at[4], pair_r.at[4], partner)
    sent.append(pair_a)
    relay(1)

    loads[3].wait()
    pair_g.wait_recv()

    @pl.when(tm < 31)
    def _():
        for core in range(2):
            pltpu.make_async_copy(grads.at[pl.ds(2, 2), core], grads.at[pl.ds(2, 2), core], halo_r.at[core]).wait()

    pair_a.wait_recv()

    def frames(start, count):
        return grads[start : start + count].reshape(count * 160, 256)

    for k in range(3):
        for h in range(2):
            tsum[pl.ds(k * 512 + h * 256, 256)] = dot(acts[h], frames(2 - k, 2), 0, 0)

    @pl.when(tm == 0)
    def _():
        for h in range(2):
            first_acts = acts[h, 0:160]
            zero = dot(first_acts, frames(0, 1), 0, 0)
            tsum[pl.ds(h * 256, 256)] += zero + dot(first_acts, frames(1, 1), 0, 0)
            tsum[pl.ds(512 + h * 256, 256)] += zero

    tsend[...] = tsum[...].astype(BF16)
    spread = []
    for at, (px, py) in enumerate(plane):
        block = 4 * py + px
        spread.append(
            send(tsend.at[rows(block, 96)], trecv.at[at], rs_s.at[at], rs_r.at[at], place(px, py, z, c))
        )
    sent += spread

    all_here(1)
    for h in range(2):
        total = dot(frames(2, 2), wt[pl.ds(h * 256, 256)], 1, 1)
        total += dot(frames(1, 2), wt[pl.ds(512 + h * 256, 256)], 1, 1)
        total += dot(frames(0, 2), wt[pl.ds(1024 + h * 256, 256)], 1, 1)
        gap[h] = total

    @pl.when(tm == 0)
    def _():
        for h in range(2):
            more = dot(frames(0, 1), wt[pl.ds(h * 256, 256)], 1, 1)
            more += dot(frames(1, 1), wt[pl.ds(h * 256, 256)], 1, 1)
            more += dot(frames(0, 1), wt[pl.ds(512 + h * 256, 256)], 1, 1)
            gap[h, 0:160] += more

    pair_p = send(gap.at[other], gap_in, pair_s.at[5], pair_r.at[5], partner)
    sent.append(pair_p)

    pair_p.wait_recv()
    for f in range(2):
        for i in range(2):
            block = pl.ds((f * 2 + i) * 80, 80)
            ga[1 + i, f] = (gap[c, block] + gap_in[block]).astype(BF16)
    row_down = pltpu.make_async_remote_copy(
        src_ref=ga.at[2],
        dst_ref=ga.at[0],
        send_sem=halo_s.at[3],
        recv_sem=halo_r.at[3],
        device_id=(tm, next_chip * 2 + c),
        device_id_type=MESH,
    )

    @pl.when(chip < 7)
    def _():
        row_down.start()

    for copy in spread:
        copy.wait_recv()
    block_sum = tsend[rows(4 * y + x, 96)].astype(F32)
    for at in range(15):
        block_sum += trecv[at].astype(F32)
    for q in range(4):
        near[q] = block_sum[48 * (q // 2) : 48 * (q // 2) + 48, 128 * (q % 2) : 128 * (q % 2) + 128].astype(BF16)
    near_copies = []
    for j in range(1, 4):
        to = lax.rem(zr + j, 4)
        near_copies.append(
            send(near.at[to], near_in.at[zr], near_s.at[j], near_r.at[j], place(x, y, 4 * zq + to, c))
        )
    sent += near_copies
    near_in[zr] = near[zr]

    @pl.when(chip == 0)
    def _():
        ga[0] = jnp.zeros_like(ga[0])

    @pl.when(chip > 0)
    def _():
        row_down.wait_recv()

    for row in range(3):
        for f in range(2):
            moved = jnp.where(first, 0.0, pltpu.roll(ga[row, f].astype(F32), 1, 0))
            shifted[row, f] = moved.astype(BF16)

    def tap(r, s):
        return ws[pl.ds((3 * r + s) * 256, 256)]

    cur, prev = ga[1:3].reshape(320, 256), ga[0:2].reshape(320, 256)
    cur_s, prev_s = shifted[1:3].reshape(320, 256), shifted[0:2].reshape(320, 256)

    def put(kind, value):
        po[0, kind] = value[:160]
        po[1, kind] = value[160:]

    put(0, dot(cur, tap(0, 0), 1, 1) + dot(cur_s, tap(0, 2), 1, 1) + dot(prev, tap(2, 0), 1, 1) + dot(prev_s, tap(2, 2), 1, 1))
    put(1, dot(cur, tap(0, 1), 1, 1) + dot(prev, tap(2, 1), 1, 1))
    put(2, dot(cur, tap(1, 0), 1, 1) + dot(cur_s, tap(1, 2), 1, 1))
    put(3, dot(cur, tap(1, 1), 1, 1))
    pair_o = send(po.at[other], po_in, pair_s.at[6], pair_r.at[6], partner)
    sent.append(pair_o)

    for copy in near_copies:
        copy.wait_recv()
    group_sum = near_in[0].astype(F32)
    for at in range(1, 4):
        group_sum += near_in[at].astype(F32)
    far[zq] = group_sum.astype(BF16)
    met(2)
    far_copies = []
    for j in range(1, 4):
        to = lax.rem(zq + j, 4)
        far_copies.append(
            send(far.at[zq], far.at[zq], far_s.at[j], far_r.at[j], place(x, y, 4 * to + zr, c))
        )
    sent += far_copies

    def finish(f, r):
        block = pl.ds(f * 80, 80)
        for lane in range(2):
            across = pl.ds(128 * lane, 128)
            for odd in range(2):
                kind = 2 * r + odd
                wide[lane, pl.ds(odd, 80, 2), :] = po[c, kind, block, across] + po_in[kind, block, across]
            outv[f, r, :, across] = wide[lane].astype(BF16)

    pair_o.wait_recv()
    for f in range(2):
        for r in range(2):
            finish(f, r)

    for copy in far_copies:
        copy.wait_recv()
    quarter = far[0].astype(F32)
    for at in range(1, 4):
        quarter += far[at].astype(F32)
    quad[...] = quarter.astype(BF16)
    fin_copies = []
    for flip in range(2):
        for j in range(4):
            if flip or j:
                to = place(jnp.bitwise_xor(x, flip), y, 4 * zq + lax.rem(zr + j, 4), xl)
                fin_copies.append(send(quad, fout.at[c, zr], fin_s.at[flip, j], fin_r.at[c, zr], to))
    here = pltpu.make_async_copy(quad, fout.at[c, zr], fin_r.at[c, zr])
    beside = pltpu.make_async_remote_copy(
        src_ref=quad, dst_ref=fout.at[c, zr], send_sem=fin_s.at[0, 0], recv_sem=fin_r.at[c, zr], device_id=partner, device_id_type=MESH
    )

    @pl.when(c == xl)
    def _():
        here.start()

    @pl.when(c != xl)
    def _():
        beside.start()

    for h in range(2):
        for q in range(4):
            pltpu.make_async_copy(fout.at[h, q], fout.at[h, q], fin_r.at[h, q]).wait()
            gt[pl.ds(48 * (q // 2), 48), pl.ds(256 * h + 128 * (q % 2), 128)] = fout[h, q].astype(F32)

    for copy in sent + fin_copies:
        copy.wait_send()

    @pl.when(c != xl)
    def _():
        beside.wait_send()

    @pl.when(tm > 0)
    def _():
        for copy in halo:
            copy.wait_send()

    @pl.when(chip > 0)
    def _():
        row_up.wait_send()

    @pl.when(chip < 7)
    def _():
        row_down.wait_send()


def local(latents, grad_out, w_spatial, w_temporal):
    dma = pltpu.SemaphoreType.DMA
    vmem = pltpu.VMEM
    return pl.pallas_call(
        kernel,
        out_shape=(
            jax.ShapeDtypeStruct(latents.shape, BF16),
            jax.ShapeDtypeStruct((96, 512), F32),
        ),
        in_specs=[pl.BlockSpec(memory_space=pl.ANY)] * 4,
        out_specs=[pl.BlockSpec(memory_space=pltpu.VMEM)] * 2,
        scratch_shapes=[
            vmem((2, 2, 160, 256), BF16),
            vmem((2304, 256), BF16),
            vmem((1536, 256), BF16),
            vmem((4, 2, 80, 256), BF16),
            vmem((5, 2, 2, 80, 256), BF16),
            vmem((2, 160, 128), F32),
            vmem((320, 2304), BF16),
            vmem((2, 320, 256), BF16),
            vmem((1536, 256), F32),
            vmem((1536, 256), BF16),
            vmem((15, 96, 256), BF16),
            vmem((144, 256), BF16),
            vmem((96, 256), BF16),
            vmem((2, 80, 256), BF16),
            vmem((4, 48, 128), BF16),
            vmem((4, 48, 128), BF16),
            vmem((4, 48, 128), BF16),
            vmem((48, 128), BF16),
            vmem((2, 4, 48, 128), BF16),
            vmem((2, 320, 256), F32),
            vmem((320, 256), F32),
            vmem((3, 2, 80, 256), BF16),
            vmem((3, 2, 80, 256), BF16),
            vmem((2, 4, 160, 256), F32),
            vmem((4, 160, 256), F32),
            dma((7,)),
            dma((7,)),
            dma((7,)),
            dma((2, 11)),
            dma((2, 11)),
            dma((2, 6)),
            dma((2, 6)),
            dma((4,)),
            dma((4,)),
            dma((15,)),
            dma((15,)),
            dma((4,)),
            dma((4,)),
            dma((4,)),
            dma((4,)),
            dma((2, 4)),
            dma((2, 4)),
            pltpu.SemaphoreType.REGULAR((3,)),
        ],
        compiler_params=pltpu.CompilerParams(
            collective_id=0, has_side_effects=True, vmem_limit_bytes=60 * 2**20
        ),
    )(latents, grad_out, w_spatial, w_temporal)


def solution(mesh):
    return jax.shard_map(
        local,
        mesh=mesh,
        in_specs=(
            P("tm", "space", None, None),
            P("tm", "space", None, None),
            P("space", None),
            P("space", None),
        ),
        out_specs=(P("tm", "space", None, None), P("space", None)),
        check_vma=False,
    )
```

```python
import jax
import jax.numpy as jnp
from jax import lax
from jax.experimental import pallas as pl
from jax.experimental.pallas import tpu as pltpu
from jax.sharding import PartitionSpec as P

MESH = pl.DeviceIdType.MESH
F32 = jnp.float32
BF16 = jnp.bfloat16
FAR = (2, 5, 7, 6)
NEAR = (4, 1, 3)


def dot(a, b, ca, cb):
    return lax.dot_general(a, b, (((ca,), (cb,)), ((), ())), preferred_element_type=F32)


def place(x, y, z, c):
    return (lax.rem(x, 2) * 16 + z, y * 4 + (x // 2) * 2 + c)


def kernel(
    lat_hbm, gout_hbm, ws_hbm, wt_hbm, outv, gt,
    lat, ws, wt, grads, eo, wide, patches, acts, tsum, tsend, trecv,
    ws_other, wt_other, g_other, near, near_in, far, quad, fout, gap, gap_in, ga, shifted, po, po_in,
    loc_sem, pair_s, pair_r, ext_s, ext_r, rel_s, rel_r, halo_s, halo_r,
    rs_s, rs_r, near_s, near_r, far_s, far_r, fin_s, fin_r, known,
):
    tm, sp = lax.axis_index("tm"), lax.axis_index("space")
    xl, z = tm // 16, lax.rem(tm, 16)
    c, chip = lax.rem(sp, 2), sp // 2
    y, xh = chip // 2, lax.rem(chip, 2)
    x = 2 * xh + xl
    par = lax.rem(xl + xh + z, 2)
    other = 1 - c
    z_up, z_down = lax.rem(z + 1, 16), lax.rem(z + 15, 16)

    partner = place(x, y, z, other)
    ups = [place(x, y, z_up, c), place(x, y, z_down, c), place(jnp.bitwise_xor(x, 1), y, z, c)]
    zq, zr = z // 4, lax.rem(z, 4)
    plane = []
    for dy in range(4):
        for dx in range(4):
            if dx or dy:
                plane.append((lax.rem(x + dx, 4), lax.rem(y + dy, 4)))
    tm_next, tm_prev = lax.rem(tm + 1, 32), lax.rem(tm + 31, 32)

    def half(index):
        return pl.ds(pl.multiple_of(index * 256, 256), 256)

    def rows(index, count):
        return pl.ds(pl.multiple_of(index * count, count), count)

    def ext_device(r):
        dxo, dy = r // 4, r % 4
        tx = 3 - x if dxo else x
        return place(tx, lax.rem(y + dy, 4), z, c)

    prev_chip = lax.rem(chip + 7, 8)
    next_chip = lax.rem(chip + 1, 8)
    loads = [
        pltpu.make_async_copy(ws_hbm.at[:, half(c)], ws.at[rows(sp, 144)], loc_sem.at[0]),
        pltpu.make_async_copy(wt_hbm.at[:, half(c)], wt.at[rows(sp, 96)], loc_sem.at[1]),
        pltpu.make_async_copy(lat_hbm, lat, loc_sem.at[2]),
        pltpu.make_async_copy(gout_hbm.at[:, 0, :, half(c)], grads.at[pl.ds(0, 2), c], loc_sem.at[3]),
        pltpu.make_async_copy(ws_hbm.at[:, half(other)], ws_other, loc_sem.at[4]),
        pltpu.make_async_copy(wt_hbm.at[:, half(other)], wt_other, loc_sem.at[5]),
        pltpu.make_async_copy(gout_hbm.at[:, 0, :, half(other)], g_other, loc_sem.at[6]),
    ]
    for at in (4, 0, 2, 5, 1, 6, 3):
        loads[at].start()

    barrier = pltpu.get_barrier_semaphore()
    xs = jnp.bitwise_xor(x, 1)
    greeted = [partner, *ups, place(xs, y, z, other), (tm_next, sp), (tm_next, chip * 2 + other)]
    greeted += [(tm, next_chip * 2 + c)] + [ext_device(r) for r in range(1, 8)]
    for device in greeted:
        pl.semaphore_signal(barrier, inc=1, device_id=device, device_id_type=MESH)
    pl.semaphore_wait(barrier, len(greeted))

    def meet(stage):
        for way in (1, -1):
            there = place(x, y, lax.rem(z + 16 + way * 2**stage, 16), c)
            pl.semaphore_signal(known.at[stage], inc=1, device_id=there, device_id_type=MESH)

    def met(stage):
        pl.semaphore_wait(known.at[stage], 2)

    meet(0)
    sent = []

    def send(src, dst, ssem, rsem, device):
        copy = pltpu.make_async_remote_copy(
            src_ref=src, dst_ref=dst, send_sem=ssem, recv_sem=rsem, device_id=device, device_id_type=MESH
        )
        copy.start()
        return copy

    loads[4].wait()
    pair_ws = send(ws_other, ws.at[rows(sp, 144)], pair_s.at[0], pair_r.at[0], partner)
    loads[5].wait()
    pair_wt = send(wt_other, wt.at[rows(sp, 96)], pair_s.at[1], pair_r.at[1], partner)

    def piece_chip(r):
        dxo, dy = r // 4, r % 4
        return lax.rem(y + 4 - dy, 4) * 2 + jnp.bitwise_xor(xh, dxo)

    weights = ((ws, 144), (wt, 96))

    def piece(which, index, part=None):
        buf, count = weights[which]
        if part is None:
            return buf.at[rows(index, count)]
        third = count // 3
        return buf.at[pl.ds(pl.multiple_of(index * count + part * third, third), third)]

    def ext_copies(which, group):
        jobs = [(r, r) for r in FAR + NEAR] if group == 0 else [(r, 8 + at) for at, r in enumerate(NEAR)]
        ref = piece(which, chip * 2 + (par if group == 0 else 1 - par))
        return [
            pltpu.make_async_remote_copy(
                src_ref=ref,
                dst_ref=ref,
                send_sem=ext_s.at[which, slot],
                recv_sem=ext_r.at[which, slot],
                device_id=ext_device(r),
                device_id_type=MESH,
            )
            for r, slot in jobs
        ]

    ext = [[ext_copies(which, group) for group in range(2)] for which in range(2)]
    for which in range(2):
        for group in range(2):
            sent += ext[which][group]
    loads[0].wait()

    def start_ext(condition, group):
        @pl.when(condition)
        def _():
            for copy in ext[0][group]:
                copy.start()

    start_ext(c == par, 0)
    start_ext(c != par, 1)
    pair_ws.wait_recv()
    start_ext(c != par, 0)
    start_ext(c == par, 1)

    loads[6].wait()
    pair_g = send(g_other, grads.at[pl.ds(0, 2), c], pair_s.at[2], pair_r.at[2], partner)
    sent += [pair_ws, pair_wt, pair_g]

    halo = []
    for h in range(2):
        halo.append(
            pltpu.make_async_remote_copy(
                src_ref=gout_hbm.at[:, 0, :, pl.ds(256 * h, 256)],
                dst_ref=grads.at[pl.ds(2, 2), c],
                send_sem=halo_s.at[h],
                recv_sem=halo_r.at[c],
                device_id=(tm_prev, chip * 2 + h),
                device_id_type=MESH,
            )
        )

    @pl.when(tm > 0)
    def _():
        for copy in halo:
            copy.start()

    met(0)
    meet(1)

    loads[2].wait()
    for f in range(2):
        for r in range(2):
            for lane in range(2):
                across = pl.ds(128 * lane, 128)
                wide[lane] = lat[f, r, :, across].astype(F32)
                for odd in range(2):
                    eo[2 * c + r, f, odd, :, across] = wide[lane, pl.ds(odd, 80, 2), :].astype(BF16)
    pair_eo = send(eo.at[pl.ds(2 * c, 2)], eo.at[pl.ds(2 * c, 2)], pair_s.at[3], pair_r.at[3], partner)
    sent.append(pair_eo)
    pair_eo.wait_recv()

    row_up = pltpu.make_async_remote_copy(
        src_ref=eo.at[0, c],
        dst_ref=eo.at[4, c],
        send_sem=halo_s.at[2],
        recv_sem=halo_r.at[2],
        device_id=(tm, prev_chip * 2 + c),
        device_id_type=MESH,
    )

    @pl.when(chip > 0)
    def _():
        row_up.start()

    @pl.when(chip == 7)
    def _():
        eo[4] = jnp.zeros_like(eo[4])

    @pl.when(tm == 31)
    def _():
        grads[2:4] = jnp.zeros_like(grads[2:4])

    last = lax.broadcasted_iota(jnp.int32, (80, 256), 0) == 79
    first = lax.broadcasted_iota(jnp.int32, (80, 256), 0) == 0

    def place_patch(f, i, r):
        row = 2 * i + r
        block = pl.ds((f * 2 + i) * 80, 80)
        even = eo[row, f, 0]
        moved = jnp.where(last, 0.0, pltpu.roll(even.astype(F32), 79, 0)).astype(BF16)
        patches[block, pl.ds(3 * r * 256, 256)] = even
        patches[block, pl.ds((3 * r + 1) * 256, 256)] = eo[row, f, 1]
        patches[block, pl.ds((3 * r + 2) * 256, 256)] = moved

    for f in range(2):
        for i in range(2):
            for r in range(3):
                if 2 * i + r < 4:
                    place_patch(f, i, r)

    met(1)
    meet(2)

    def relay(which):
        for at, r in enumerate(FAR):
            ext[which][0][at].wait_recv()
            index = piece_chip(r) * 2 + par
            for part in range(3):
                ref = piece(which, index, part) if at == 3 else piece(which, index)
                if at == 3 or part == at:
                    slot = 3 + part if at == 3 else at
                    sent.append(send(ref, ref, rel_s.at[which, slot], rel_r.at[which, slot], ups[part]))

    def all_here(which):
        for copy in ext[which][0][4:] + ext[which][1]:
            copy.wait_recv()
        for at, r in enumerate(FAR):
            index = piece_chip(r) * 2 + 1 - par
            if at < 3:
                ref = piece(which, index)
                pltpu.make_async_copy(ref, ref, rel_r.at[which, at]).wait()
            else:
                for part in range(3):
                    ref = piece(which, index, part)
                    pltpu.make_async_copy(ref, ref, rel_r.at[which, 3 + part]).wait()

    row_pair = pltpu.make_async_remote_copy(
        src_ref=eo.at[4, c],
        dst_ref=eo.at[4, c],
        send_sem=pair_s.at[7],
        recv_sem=pair_r.at[7],
        device_id=partner,
        device_id_type=MESH,
    )

    relay(0)

    @pl.when(chip < 7)
    def _():
        row_up.wait_recv()
        row_pair.start()

    loads[1].wait()
    pair_wt.wait_recv()
    for copy in ext[1][0] + ext[1][1]:
        copy.start()

    @pl.when(chip < 7)
    def _():
        row_pair.wait_recv()

    for f in range(2):
        place_patch(f, 1, 2)
    all_here(0)

    acts[c] = jnp.dot(patches[...], ws[...], preferred_element_type=F32).astype(BF16)
    pair_a = send(acts.at[c], acts.at[c], pair_s.at[4], pair_r.at[4], partner)
    sent.append(pair_a)

    loads[3].wait()
    pair_g.wait_recv()

    @pl.when(tm < 31)
    def _():
        for core in range(2):
            pltpu.make_async_copy(grads.at[pl.ds(2, 2), core], grads.at[pl.ds(2, 2), core], halo_r.at[core]).wait()

    pair_a.wait_recv()

    def frames(start, count):
        return grads[start : start + count].reshape(count * 160, 256)

    for k in range(3):
        for h in range(2):
            tsum[pl.ds(k * 512 + h * 256, 256)] = dot(acts[h], frames(2 - k, 2), 0, 0)

    @pl.when(tm == 0)
    def _():
        for h in range(2):
            first_acts = acts[h, 0:160]
            zero = dot(first_acts, frames(0, 1), 0, 0)
            tsum[pl.ds(h * 256, 256)] += zero + dot(first_acts, frames(1, 1), 0, 0)
            tsum[pl.ds(512 + h * 256, 256)] += zero

    tsend[...] = tsum[...].astype(BF16)
    spread = []
    for at, (px, py) in enumerate(plane):
        block = 4 * py + px
        spread.append(
            send(tsend.at[rows(block, 96)], trecv.at[at], rs_s.at[at], rs_r.at[at], place(px, py, z, c))
        )
    sent += spread

    relay(1)
    all_here(1)
    for h in range(2):
        total = dot(frames(2, 2), wt[pl.ds(h * 256, 256)], 1, 1)
        total += dot(frames(1, 2), wt[pl.ds(512 + h * 256, 256)], 1, 1)
        total += dot(frames(0, 2), wt[pl.ds(1024 + h * 256, 256)], 1, 1)
        gap[h] = total

    @pl.when(tm == 0)
    def _():
        for h in range(2):
            more = dot(frames(0, 1), wt[pl.ds(h * 256, 256)], 1, 1)
            more += dot(frames(1, 1), wt[pl.ds(h * 256, 256)], 1, 1)
            more += dot(frames(0, 1), wt[pl.ds(512 + h * 256, 256)], 1, 1)
            gap[h, 0:160] += more

    pair_p = send(gap.at[other], gap_in, pair_s.at[5], pair_r.at[5], partner)
    sent.append(pair_p)

    pair_p.wait_recv()
    for f in range(2):
        for i in range(2):
            block = pl.ds((f * 2 + i) * 80, 80)
            ga[1 + i, f] = (gap[c, block] + gap_in[block]).astype(BF16)
    row_down = pltpu.make_async_remote_copy(
        src_ref=ga.at[2],
        dst_ref=ga.at[0],
        send_sem=halo_s.at[3],
        recv_sem=halo_r.at[3],
        device_id=(tm, next_chip * 2 + c),
        device_id_type=MESH,
    )

    @pl.when(chip < 7)
    def _():
        row_down.start()

    for copy in spread:
        copy.wait_recv()
    block_sum = tsend[rows(4 * y + x, 96)].astype(F32)
    for at in range(15):
        block_sum += trecv[at].astype(F32)
    for q in range(4):
        near[q] = block_sum[48 * (q // 2) : 48 * (q // 2) + 48, 128 * (q % 2) : 128 * (q % 2) + 128].astype(BF16)
    near_copies = []
    for j in range(1, 4):
        to = lax.rem(zr + j, 4)
        near_copies.append(
            send(near.at[to], near_in.at[zr], near_s.at[j], near_r.at[j], place(x, y, 4 * zq + to, c))
        )
    sent += near_copies
    near_in[zr] = near[zr]

    @pl.when(chip == 0)
    def _():
        ga[0] = jnp.zeros_like(ga[0])

    @pl.when(chip > 0)
    def _():
        row_down.wait_recv()

    for row in range(3):
        for f in range(2):
            moved = jnp.where(first, 0.0, pltpu.roll(ga[row, f].astype(F32), 1, 0))
            shifted[row, f] = moved.astype(BF16)

    def tap(r, s):
        return ws[pl.ds((3 * r + s) * 256, 256)]

    cur, prev = ga[1:3].reshape(320, 256), ga[0:2].reshape(320, 256)
    cur_s, prev_s = shifted[1:3].reshape(320, 256), shifted[0:2].reshape(320, 256)

    def put(kind, value):
        po[0, kind] = value[:160]
        po[1, kind] = value[160:]

    put(0, dot(cur, tap(0, 0), 1, 1) + dot(cur_s, tap(0, 2), 1, 1) + dot(prev, tap(2, 0), 1, 1) + dot(prev_s, tap(2, 2), 1, 1))
    put(1, dot(cur, tap(0, 1), 1, 1) + dot(prev, tap(2, 1), 1, 1))
    put(2, dot(cur, tap(1, 0), 1, 1) + dot(cur_s, tap(1, 2), 1, 1))
    put(3, dot(cur, tap(1, 1), 1, 1))
    pair_o = send(po.at[other], po_in, pair_s.at[6], pair_r.at[6], partner)
    sent.append(pair_o)

    for copy in near_copies:
        copy.wait_recv()
    group_sum = near_in[0].astype(F32)
    for at in range(1, 4):
        group_sum += near_in[at].astype(F32)
    far[zq] = group_sum.astype(BF16)
    met(2)
    far_copies = []
    for j in range(1, 4):
        to = lax.rem(zq + j, 4)
        far_copies.append(
            send(far.at[zq], far.at[zq], far_s.at[j], far_r.at[j], place(x, y, 4 * to + zr, c))
        )
    sent += far_copies

    def finish(f, r):
        block = pl.ds(f * 80, 80)
        for lane in range(2):
            across = pl.ds(128 * lane, 128)
            for odd in range(2):
                kind = 2 * r + odd
                wide[lane, pl.ds(odd, 80, 2), :] = po[c, kind, block, across] + po_in[kind, block, across]
            outv[f, r, :, across] = wide[lane].astype(BF16)

    pair_o.wait_recv()
    for f in range(2):
        for r in range(2):
            finish(f, r)

    for copy in far_copies:
        copy.wait_recv()
    quarter = far[0].astype(F32)
    for at in range(1, 4):
        quarter += far[at].astype(F32)
    quad[...] = quarter.astype(BF16)
    fin_copies = []
    for flip in range(2):
        for j in range(4):
            if flip or j:
                to = place(jnp.bitwise_xor(x, flip), y, 4 * zq + lax.rem(zr + j, 4), xl)
                fin_copies.append(send(quad, fout.at[c, zr], fin_s.at[flip, j], fin_r.at[c, zr], to))
    here = pltpu.make_async_copy(quad, fout.at[c, zr], fin_r.at[c, zr])
    beside = pltpu.make_async_remote_copy(
        src_ref=quad, dst_ref=fout.at[c, zr], send_sem=fin_s.at[0, 0], recv_sem=fin_r.at[c, zr], device_id=partner, device_id_type=MESH
    )

    @pl.when(c == xl)
    def _():
        here.start()

    @pl.when(c != xl)
    def _():
        beside.start()

    for h in range(2):
        for q in range(4):
            pltpu.make_async_copy(fout.at[h, q], fout.at[h, q], fin_r.at[h, q]).wait()
            gt[pl.ds(48 * (q // 2), 48), pl.ds(256 * h + 128 * (q % 2), 128)] = fout[h, q].astype(F32)

    for copy in sent + fin_copies:
        copy.wait_send()

    @pl.when(c != xl)
    def _():
        beside.wait_send()

    @pl.when(tm > 0)
    def _():
        for copy in halo:
            copy.wait_send()

    @pl.when(chip > 0)
    def _():
        row_up.wait_send()

    @pl.when(chip < 7)
    def _():
        row_pair.wait_send()

    @pl.when(chip < 7)
    def _():
        row_down.wait_send()


def local(latents, grad_out, w_spatial, w_temporal):
    dma = pltpu.SemaphoreType.DMA
    vmem = pltpu.VMEM
    return pl.pallas_call(
        kernel,
        out_shape=(
            pltpu.VMEM(latents.shape, BF16),
            pltpu.VMEM((96, 512), F32),
        ),
        in_specs=[pl.BlockSpec(memory_space=pl.ANY)] * 4,
        scratch_shapes=[
            vmem((2, 2, 160, 256), BF16),
            vmem((2304, 256), BF16),
            vmem((1536, 256), BF16),
            vmem((4, 2, 80, 256), BF16),
            vmem((5, 2, 2, 80, 256), BF16),
            vmem((2, 160, 128), F32),
            vmem((320, 2304), BF16),
            vmem((2, 320, 256), BF16),
            vmem((1536, 256), F32),
            vmem((1536, 256), BF16),
            vmem((15, 96, 256), BF16),
            vmem((144, 256), BF16),
            vmem((96, 256), BF16),
            vmem((2, 80, 256), BF16),
            vmem((4, 48, 128), BF16),
            vmem((4, 48, 128), BF16),
            vmem((4, 48, 128), BF16),
            vmem((48, 128), BF16),
            vmem((2, 4, 48, 128), BF16),
            vmem((2, 320, 256), F32),
            vmem((320, 256), F32),
            vmem((3, 2, 80, 256), BF16),
            vmem((3, 2, 80, 256), BF16),
            vmem((2, 4, 160, 256), F32),
            vmem((4, 160, 256), F32),
            dma((7,)),
            dma((8,)),
            dma((8,)),
            dma((2, 11)),
            dma((2, 11)),
            dma((2, 6)),
            dma((2, 6)),
            dma((4,)),
            dma((4,)),
            dma((15,)),
            dma((15,)),
            dma((4,)),
            dma((4,)),
            dma((4,)),
            dma((4,)),
            dma((2, 4)),
            dma((2, 4)),
            pltpu.SemaphoreType.REGULAR((3,)),
        ],
        compiler_params=pltpu.CompilerParams(
            collective_id=0, has_side_effects=True, vmem_limit_bytes=60 * 2**20
        ),
    )(latents, grad_out, w_spatial, w_temporal)


def solution(mesh):
    return jax.shard_map(
        local,
        mesh=mesh,
        in_specs=(
            P("tm", "space", None, None),
            P("tm", "space", None, None),
            P("space", None),
            P("space", None),
        ),
        out_specs=(P("tm", "space", None, None), P("space", None)),
        check_vma=False,
    )
```

```python
import jax
import jax.numpy as jnp
from jax import lax
from jax.experimental import pallas as pl
from jax.experimental.pallas import tpu as pltpu
from jax.sharding import PartitionSpec as P

MESH = pl.DeviceIdType.MESH
F32 = jnp.float32
BF16 = jnp.bfloat16
FAR = (2, 5, 7, 6)
NEAR = (4, 1, 3)


def dot(a, b, ca, cb):
    return lax.dot_general(a, b, (((ca,), (cb,)), ((), ())), preferred_element_type=F32)


def place(x, y, z, c):
    return (lax.rem(x, 2) * 16 + z, y * 4 + (x // 2) * 2 + c)


def kernel(
    lat_hbm, gout_hbm, ws_hbm, wt_hbm, outv, gt,
    lat, ws, wt, grads, eo, wide, patches, acts, tsend, trecv,
    ws_other, wt_other, g_other, near, near_in, far, quad, fout, gap, gap_in, ga, shifted, po, po_in,
    loc_sem, pair_s, pair_r, ext_s, ext_r, rel_s, rel_r, halo_s, halo_r,
    rs_s, rs_r, near_s, near_r, far_s, far_r, fin_s, fin_r, known,
):
    tm, sp = lax.axis_index("tm"), lax.axis_index("space")
    xl, z = tm // 16, lax.rem(tm, 16)
    c, chip = lax.rem(sp, 2), sp // 2
    y, xh = chip // 2, lax.rem(chip, 2)
    x = 2 * xh + xl
    par = lax.rem(xl + xh + z, 2)
    other = 1 - c
    z_up, z_down = lax.rem(z + 1, 16), lax.rem(z + 15, 16)

    partner = place(x, y, z, other)
    ups = [place(x, y, z_up, c), place(x, y, z_down, c), place(jnp.bitwise_xor(x, 1), y, z, c)]
    zq, zr = z // 4, lax.rem(z, 4)
    plane = []
    for dy in range(4):
        for dx in range(4):
            if dx or dy:
                plane.append((min(dx, 4 - dx) + min(dy, 4 - dy), lax.rem(x + dx, 4), lax.rem(y + dy, 4)))
    plane = [entry[1:] for entry in sorted(plane, key=lambda entry: -entry[0])]
    tm_next, tm_prev = lax.rem(tm + 1, 32), lax.rem(tm + 31, 32)

    def half(index):
        return pl.ds(pl.multiple_of(index * 256, 256), 256)

    def rows(index, count):
        return pl.ds(pl.multiple_of(index * count, count), count)

    def ext_device(r):
        dxo, dy = r // 4, r % 4
        tx = 3 - x if dxo else x
        return place(tx, lax.rem(y + dy, 4), z, c)

    prev_chip = lax.rem(chip + 7, 8)
    next_chip = lax.rem(chip + 1, 8)
    loads = [
        pltpu.make_async_copy(ws_hbm.at[:, half(c)], ws.at[rows(sp, 144)], loc_sem.at[0]),
        pltpu.make_async_copy(wt_hbm.at[:, half(c)], wt.at[rows(sp, 96)], loc_sem.at[1]),
        pltpu.make_async_copy(lat_hbm, lat, loc_sem.at[2]),
        pltpu.make_async_copy(gout_hbm.at[:, 0, :, half(c)], grads.at[pl.ds(0, 2), c], loc_sem.at[3]),
        pltpu.make_async_copy(ws_hbm.at[:, half(other)], ws_other, loc_sem.at[4]),
        pltpu.make_async_copy(wt_hbm.at[:, half(other)], wt_other, loc_sem.at[5]),
        pltpu.make_async_copy(gout_hbm.at[:, 0, :, half(other)], g_other, loc_sem.at[6]),
    ]
    for at in (4, 0, 2, 5, 1, 6, 3):
        loads[at].start()

    barrier = pltpu.get_barrier_semaphore()
    xs = jnp.bitwise_xor(x, 1)
    greeted = [partner, *ups, place(xs, y, z, other), (tm_next, sp), (tm_next, chip * 2 + other)]
    greeted += [(tm, next_chip * 2 + c)] + [ext_device(r) for r in range(1, 8)]
    for device in greeted:
        pl.semaphore_signal(barrier, inc=1, device_id=device, device_id_type=MESH)
    pl.semaphore_wait(barrier, len(greeted))

    def meet(stage):
        for way in (1, -1):
            there = place(x, y, lax.rem(z + 16 + way * 2**stage, 16), c)
            pl.semaphore_signal(known.at[stage], inc=1, device_id=there, device_id_type=MESH)

    def met(stage):
        pl.semaphore_wait(known.at[stage], 2)

    meet(0)
    sent = []

    def send(src, dst, ssem, rsem, device):
        copy = pltpu.make_async_remote_copy(
            src_ref=src, dst_ref=dst, send_sem=ssem, recv_sem=rsem, device_id=device, device_id_type=MESH
        )
        copy.start()
        return copy

    loads[4].wait()
    pair_ws = send(ws_other, ws.at[rows(sp, 144)], pair_s.at[0], pair_r.at[0], partner)
    loads[5].wait()
    pair_wt = send(wt_other, wt.at[rows(sp, 96)], pair_s.at[1], pair_r.at[1], partner)

    def piece_chip(r):
        dxo, dy = r // 4, r % 4
        return lax.rem(y + 4 - dy, 4) * 2 + jnp.bitwise_xor(xh, dxo)

    weights = ((ws, 144), (wt, 96))

    def piece(which, index, part=None):
        buf, count = weights[which]
        if part is None:
            return buf.at[rows(index, count)]
        third = count // 3
        return buf.at[pl.ds(pl.multiple_of(index * count + part * third, third), third)]

    def ext_copies(which, group):
        jobs = [(r, r) for r in FAR + NEAR] if group == 0 else [(r, 8 + at) for at, r in enumerate(NEAR)]
        ref = piece(which, chip * 2 + (par if group == 0 else 1 - par))
        return [
            pltpu.make_async_remote_copy(
                src_ref=ref,
                dst_ref=ref,
                send_sem=ext_s.at[which, slot],
                recv_sem=ext_r.at[which, slot],
                device_id=ext_device(r),
                device_id_type=MESH,
            )
            for r, slot in jobs
        ]

    ext = [[ext_copies(which, group) for group in range(2)] for which in range(2)]
    for which in range(2):
        for group in range(2):
            sent += ext[which][group]
    loads[0].wait()

    def start_ext(condition, group):
        @pl.when(condition)
        def _():
            for copy in ext[0][group]:
                copy.start()

    start_ext(c == par, 0)
    start_ext(c != par, 1)
    pair_ws.wait_recv()
    start_ext(c != par, 0)
    start_ext(c == par, 1)

    loads[6].wait()
    pair_g = send(g_other, grads.at[pl.ds(0, 2), c], pair_s.at[2], pair_r.at[2], partner)
    sent += [pair_ws, pair_wt, pair_g]

    halo = []
    for h in range(2):
        halo.append(
            pltpu.make_async_remote_copy(
                src_ref=gout_hbm.at[:, 0, :, pl.ds(256 * h, 256)],
                dst_ref=grads.at[pl.ds(2, 2), c],
                send_sem=halo_s.at[h],
                recv_sem=halo_r.at[c],
                device_id=(tm_prev, chip * 2 + h),
                device_id_type=MESH,
            )
        )

    @pl.when(tm > 0)
    def _():
        for copy in halo:
            copy.start()

    met(0)
    meet(1)

    loads[2].wait()
    for f in range(2):
        for r in range(2):
            for lane in range(2):
                across = pl.ds(128 * lane, 128)
                wide[lane] = lat[f, r, :, across].astype(F32)
                for odd in range(2):
                    eo[2 * c + r, f, odd, :, across] = wide[lane, pl.ds(odd, 80, 2), :].astype(BF16)
    pair_eo = send(eo.at[pl.ds(2 * c, 2)], eo.at[pl.ds(2 * c, 2)], pair_s.at[3], pair_r.at[3], partner)
    sent.append(pair_eo)
    pair_eo.wait_recv()

    row_up = pltpu.make_async_remote_copy(
        src_ref=eo.at[0, c],
        dst_ref=eo.at[4, c],
        send_sem=halo_s.at[2],
        recv_sem=halo_r.at[2],
        device_id=(tm, prev_chip * 2 + c),
        device_id_type=MESH,
    )

    @pl.when(chip > 0)
    def _():
        row_up.start()

    @pl.when(chip == 7)
    def _():
        eo[4] = jnp.zeros_like(eo[4])

    @pl.when(tm == 31)
    def _():
        grads[2:4] = jnp.zeros_like(grads[2:4])

    last = lax.broadcasted_iota(jnp.int32, (80, 256), 0) == 79
    first = lax.broadcasted_iota(jnp.int32, (80, 256), 0) == 0

    def place_patch(f, i, r):
        row = 2 * i + r
        block = pl.ds((f * 2 + i) * 80, 80)
        even = eo[row, f, 0]
        moved = jnp.where(last, 0.0, pltpu.roll(even.astype(F32), 79, 0)).astype(BF16)
        patches[block, pl.ds(3 * r * 256, 256)] = even
        patches[block, pl.ds((3 * r + 1) * 256, 256)] = eo[row, f, 1]
        patches[block, pl.ds((3 * r + 2) * 256, 256)] = moved

    for f in range(2):
        for i in range(2):
            for r in range(3):
                if 2 * i + r < 4:
                    place_patch(f, i, r)

    met(1)
    meet(2)

    def relay(which):
        for at, r in enumerate(FAR):
            ext[which][0][at].wait_recv()
            index = piece_chip(r) * 2 + par
            for part in range(3):
                ref = piece(which, index, part) if at == 3 else piece(which, index)
                if at == 3 or part == at:
                    slot = 3 + part if at == 3 else at
                    sent.append(send(ref, ref, rel_s.at[which, slot], rel_r.at[which, slot], ups[part]))

    def all_here(which):
        for copy in ext[which][0][4:] + ext[which][1]:
            copy.wait_recv()
        for at, r in enumerate(FAR):
            index = piece_chip(r) * 2 + 1 - par
            if at < 3:
                ref = piece(which, index)
                pltpu.make_async_copy(ref, ref, rel_r.at[which, at]).wait()
            else:
                for part in range(3):
                    ref = piece(which, index, part)
                    pltpu.make_async_copy(ref, ref, rel_r.at[which, 3 + part]).wait()

    row_pair = pltpu.make_async_remote_copy(
        src_ref=eo.at[4, c],
        dst_ref=eo.at[4, c],
        send_sem=pair_s.at[7],
        recv_sem=pair_r.at[7],
        device_id=partner,
        device_id_type=MESH,
    )

    relay(0)

    @pl.when(chip < 7)
    def _():
        row_up.wait_recv()
        row_pair.start()

    loads[1].wait()
    pair_wt.wait_recv()
    for copy in ext[1][0] + ext[1][1]:
        copy.start()

    @pl.when(chip < 7)
    def _():
        row_pair.wait_recv()

    for f in range(2):
        place_patch(f, 1, 2)
    all_here(0)

    acts[c] = jnp.dot(patches[...], ws[...], preferred_element_type=F32).astype(BF16)
    pair_a = send(acts.at[c], acts.at[c], pair_s.at[4], pair_r.at[4], partner)
    sent.append(pair_a)

    loads[3].wait()
    pair_g.wait_recv()

    @pl.when(tm < 31)
    def _():
        for core in range(2):
            pltpu.make_async_copy(grads.at[pl.ds(2, 2), core], grads.at[pl.ds(2, 2), core], halo_r.at[core]).wait()

    pair_a.wait_recv()

    def frames(start, count):
        return grads[start : start + count].reshape(count * 160, 256)

    def terms(starts):
        for k in range(3):
            for h in range(2):
                value = dot(acts[h], frames(2 - k, 2), 0, 0)
                for frame in range(2 - k if starts else 0):
                    value += dot(acts[h, 0:160], frames(frame, 1), 0, 0)
                tsend[pl.ds(k * 512 + h * 256, 256)] = value.astype(BF16)

    @pl.when(tm > 0)
    def _():
        terms(False)

    @pl.when(tm == 0)
    def _():
        terms(True)

    spread = []
    for at, (px, py) in enumerate(plane):
        block = 4 * py + px
        spread.append(
            send(tsend.at[rows(block, 96)], trecv.at[at], rs_s.at[at], rs_r.at[at], place(px, py, z, c))
        )
    sent += spread

    relay(1)
    all_here(1)
    for h in range(2):
        total = dot(frames(2, 2), wt[pl.ds(h * 256, 256)], 1, 1)
        total += dot(frames(1, 2), wt[pl.ds(512 + h * 256, 256)], 1, 1)
        total += dot(frames(0, 2), wt[pl.ds(1024 + h * 256, 256)], 1, 1)
        gap[h] = total

    @pl.when(tm == 0)
    def _():
        for h in range(2):
            more = dot(frames(0, 1), wt[pl.ds(h * 256, 256)], 1, 1)
            more += dot(frames(1, 1), wt[pl.ds(h * 256, 256)], 1, 1)
            more += dot(frames(0, 1), wt[pl.ds(512 + h * 256, 256)], 1, 1)
            gap[h, 0:160] += more

    pair_p = send(gap.at[other], gap_in, pair_s.at[5], pair_r.at[5], partner)
    sent.append(pair_p)

    pair_p.wait_recv()
    for f in range(2):
        for i in range(2):
            block = pl.ds((f * 2 + i) * 80, 80)
            ga[1 + i, f] = (gap[c, block] + gap_in[block]).astype(BF16)
    row_down = pltpu.make_async_remote_copy(
        src_ref=ga.at[2],
        dst_ref=ga.at[0],
        send_sem=halo_s.at[3],
        recv_sem=halo_r.at[3],
        device_id=(tm, next_chip * 2 + c),
        device_id_type=MESH,
    )

    @pl.when(chip < 7)
    def _():
        row_down.start()

    for copy in spread:
        copy.wait_recv()
    block_sum = tsend[rows(4 * y + x, 96)].astype(F32)
    for at in range(15):
        block_sum += trecv[at].astype(F32)
    for q in range(4):
        near[q] = block_sum[48 * (q // 2) : 48 * (q // 2) + 48, 128 * (q % 2) : 128 * (q % 2) + 128].astype(BF16)
    near_copies = []
    for j in range(1, 4):
        to = lax.rem(zr + j, 4)
        near_copies.append(
            send(near.at[to], near_in.at[zr], near_s.at[j], near_r.at[j], place(x, y, 4 * zq + to, c))
        )
    sent += near_copies
    near_in[zr] = near[zr]

    @pl.when(chip == 0)
    def _():
        ga[0] = jnp.zeros_like(ga[0])

    @pl.when(chip > 0)
    def _():
        row_down.wait_recv()

    for row in range(3):
        for f in range(2):
            moved = jnp.where(first, 0.0, pltpu.roll(ga[row, f].astype(F32), 1, 0))
            shifted[row, f] = moved.astype(BF16)

    def tap(r, s):
        return ws[pl.ds((3 * r + s) * 256, 256)]

    cur, prev = ga[1:3].reshape(320, 256), ga[0:2].reshape(320, 256)
    cur_s, prev_s = shifted[1:3].reshape(320, 256), shifted[0:2].reshape(320, 256)

    def put(kind, value):
        po[0, kind] = value[:160]
        po[1, kind] = value[160:]

    put(0, dot(cur, tap(0, 0), 1, 1) + dot(cur_s, tap(0, 2), 1, 1) + dot(prev, tap(2, 0), 1, 1) + dot(prev_s, tap(2, 2), 1, 1))
    put(1, dot(cur, tap(0, 1), 1, 1) + dot(prev, tap(2, 1), 1, 1))
    put(2, dot(cur, tap(1, 0), 1, 1) + dot(cur_s, tap(1, 2), 1, 1))
    put(3, dot(cur, tap(1, 1), 1, 1))
    pair_o = send(po.at[other], po_in, pair_s.at[6], pair_r.at[6], partner)
    sent.append(pair_o)

    for copy in near_copies:
        copy.wait_recv()
    group_sum = near_in[0].astype(F32)
    for at in range(1, 4):
        group_sum += near_in[at].astype(F32)
    far[zq] = group_sum.astype(BF16)
    met(2)
    far_copies = []
    for j in (2, 1, 3):
        to = lax.rem(zq + j, 4)
        far_copies.append(
            send(far.at[zq], far.at[zq], far_s.at[j], far_r.at[j], place(x, y, 4 * to + zr, c))
        )
    sent += far_copies

    def finish(f, r):
        block = pl.ds(f * 80, 80)
        for lane in range(2):
            across = pl.ds(128 * lane, 128)
            for odd in range(2):
                kind = 2 * r + odd
                wide[lane, pl.ds(odd, 80, 2), :] = po[c, kind, block, across] + po_in[kind, block, across]
            outv[f, r, :, across] = wide[lane].astype(BF16)

    pair_o.wait_recv()
    for f in range(2):
        for r in range(2):
            finish(f, r)

    for copy in far_copies:
        copy.wait_recv()
    quarter = far[0].astype(F32)
    for at in range(1, 4):
        quarter += far[at].astype(F32)
    quad[...] = quarter.astype(BF16)
    fin_copies = []
    for flip in (1, 0):
        for j in (2, 3, 1, 0):
            if flip or j:
                to = place(jnp.bitwise_xor(x, flip), y, 4 * zq + lax.rem(zr + j, 4), xl)
                fin_copies.append(send(quad, fout.at[c, zr], fin_s.at[flip, j], fin_r.at[c, zr], to))
    here = pltpu.make_async_copy(quad, fout.at[c, zr], fin_r.at[c, zr])
    beside = pltpu.make_async_remote_copy(
        src_ref=quad, dst_ref=fout.at[c, zr], send_sem=fin_s.at[0, 0], recv_sem=fin_r.at[c, zr], device_id=partner, device_id_type=MESH
    )

    @pl.when(c == xl)
    def _():
        here.start()

    @pl.when(c != xl)
    def _():
        beside.start()

    for h in range(2):
        for q in range(4):
            pltpu.make_async_copy(fout.at[h, q], fout.at[h, q], fin_r.at[h, q]).wait()
            gt[pl.ds(48 * (q // 2), 48), pl.ds(256 * h + 128 * (q % 2), 128)] = fout[h, q].astype(F32)

    for copy in sent + fin_copies:
        copy.wait_send()

    @pl.when(c != xl)
    def _():
        beside.wait_send()

    @pl.when(tm > 0)
    def _():
        for copy in halo:
            copy.wait_send()

    @pl.when(chip > 0)
    def _():
        row_up.wait_send()

    @pl.when(chip < 7)
    def _():
        row_pair.wait_send()

    @pl.when(chip < 7)
    def _():
        row_down.wait_send()


def local(latents, grad_out, w_spatial, w_temporal):
    dma = pltpu.SemaphoreType.DMA
    vmem = pltpu.VMEM
    return pl.pallas_call(
        kernel,
        out_shape=(
            pltpu.VMEM(latents.shape, BF16),
            pltpu.VMEM((96, 512), F32),
        ),
        in_specs=[pl.BlockSpec(memory_space=pl.ANY)] * 4,
        scratch_shapes=[
            vmem((2, 2, 160, 256), BF16),
            vmem((2304, 256), BF16),
            vmem((1536, 256), BF16),
            vmem((4, 2, 80, 256), BF16),
            vmem((5, 2, 2, 80, 256), BF16),
            vmem((2, 160, 128), F32),
            vmem((320, 2304), BF16),
            vmem((2, 320, 256), BF16),
            vmem((1536, 256), BF16),
            vmem((15, 96, 256), BF16),
            vmem((144, 256), BF16),
            vmem((96, 256), BF16),
            vmem((2, 80, 256), BF16),
            vmem((4, 48, 128), BF16),
            vmem((4, 48, 128), BF16),
            vmem((4, 48, 128), BF16),
            vmem((48, 128), BF16),
            vmem((2, 4, 48, 128), BF16),
            vmem((2, 320, 256), F32),
            vmem((320, 256), F32),
            vmem((3, 2, 80, 256), BF16),
            vmem((3, 2, 80, 256), BF16),
            vmem((2, 4, 160, 256), F32),
            vmem((4, 160, 256), F32),
            dma((7,)),
            dma((8,)),
            dma((8,)),
            dma((2, 11)),
            dma((2, 11)),
            dma((2, 6)),
            dma((2, 6)),
            dma((4,)),
            dma((4,)),
            dma((15,)),
            dma((15,)),
            dma((4,)),
            dma((4,)),
            dma((4,)),
            dma((4,)),
            dma((2, 4)),
            dma((2, 4)),
            pltpu.SemaphoreType.REGULAR((3,)),
        ],
        compiler_params=pltpu.CompilerParams(
            collective_id=0, has_side_effects=True, vmem_limit_bytes=60 * 2**20
        ),
    )(latents, grad_out, w_spatial, w_temporal)


def solution(mesh):
    return jax.shard_map(
        local,
        mesh=mesh,
        in_specs=(
            P("tm", "space", None, None),
            P("tm", "space", None, None),
            P("space", None),
            P("space", None),
        ),
        out_specs=(P("tm", "space", None, None), P("space", None)),
        check_vma=False,
    )
```
